256 devices in a mesh: row: 16 (over y_lo, x, core), col: 16 (over y_hi, z).
Axes of the slice: x: 4, y: 4 (y_hi: 2, y_lo: 2; y = y_hi * 2 + y_lo), z: 8, core: 2. Of those that a mesh axis runs over, the one named last changes fastest.
Arguments:
- pair_tensor: float32 [512, 512, 128], P('row', 'col'), may hold values from -6 to 6
- norm_in_gain: float32 [2, 128], replicated, may hold values from 0.5 to 1.5
- norm_in_bias: float32 [2, 128], replicated, may hold values from -3 to 3
- proj_weight: bfloat16 [2, 128, 512], replicated, may hold values from -0.5 to 0.5
- gate_weight: bfloat16 [2, 128, 128], replicated, may hold values from -0.5 to 0.5
- norm_out_gain: float32 [2, 128], replicated, may hold values from 0.5 to 1.5
- norm_out_bias: float32 [2, 128], replicated, may hold values from -3 to 3
- out_weight: bfloat16 [2, 128, 128], replicated, may hold values from -0.5 to 0.5
Outputs:
- pair_out: float32 [512, 512, 128], P('row', 'col')
The draws below stay inside these ranges and needn't reach their ends.
All inputs are finite; a program needn't handle non-finite values.
Results may differ from the reference program's by a relative error of at most 0.0023.
Values may be sent and summed in bfloat16 or wider, within the bound.
No kernel may reach another device: no remote copies, remote signals or barrier semaphores. Data moves between devices by JAX's collectives and lax.ppermute only.
A program may use at most 64 MiB of HBM per device.

```python
import jax
import jax.numpy as jnp
from jax import lax

C = 128
N = 512


def block_scale(key, shape, cuts, low, top_value):
    factor_of = 1.0
    for position, parts in cuts:
        steps = jax.random.uniform(jax.random.fold_in(jax.random.fold_in(key, 6), position), (parts,), jnp.float32, low / len(cuts), top_value / len(cuts))
        factor_of = factor_of * jnp.repeat(jnp.exp(steps), shape[position] // parts).reshape((-1,) + (1,) * (len(shape) - 1 - position))
    return factor_of


def noise(key, extent, spread, bound, cuts=(), held_as=jnp.bfloat16):
    values = spread * jax.random.normal(key, extent, jnp.float32)
    if cuts:
        values = values * block_scale(key, extent, cuts, -0.22, 0.18)
    return jnp.clip(values, -bound, bound).astype(held_as)


def setup_inputs(seed: int = 0) -> dict:
    key_list = jax.random.split(jax.random.key(seed), 9)
    pair_tensor = noise(key_list[0], (N, N, C), 1.0, 6.0, ((0, 16), (1, 16)), jnp.float32)
    norm_in_gain = jnp.clip(jax.random.uniform(key_list[1], (2, C), jnp.float32, 0.5, 1.5), 0.5, 1.5)
    norm_in_bias = noise(key_list[2], (2, C), 0.5, 3.0, (), jnp.float32)
    proj_weight = noise(key_list[3], (2, C, 4 * C), C ** -0.5, 0.5)
    gate_weight = noise(key_list[4], (2, C, C), C ** -0.5, 0.5)
    norm_out_gain = jnp.clip(jax.random.uniform(key_list[5], (2, C), jnp.float32, 0.5, 1.5), 0.5, 1.5)
    norm_out_bias = noise(key_list[6], (2, C), 0.5, 3.0, (), jnp.float32)
    out_weight = noise(key_list[7], (2, C, C), C ** -0.5, 0.5)
    return dict(pair_tensor=pair_tensor, norm_in_gain=norm_in_gain, norm_in_bias=norm_in_bias, proj_weight=proj_weight, gate_weight=gate_weight, norm_out_gain=norm_out_gain, norm_out_bias=norm_out_bias, out_weight=out_weight)


def layer_norm(values, gain_vec, bias_vec):
    average = lax.optimization_barrier(jnp.mean(values, axis=-1, keepdims=True))
    centered = values - average
    variance = lax.optimization_barrier(jnp.mean(centered * centered, axis=-1, keepdims=True))
    return centered * jax.lax.rsqrt(variance + 1e-05) * gain_vec + bias_vec

def triangle(pair_tensor, layer, norm_in_gain, norm_in_bias, proj_weight, gate_weight, norm_out_gain, norm_out_bias, out_weight):
    width = pair_tensor.shape[-1]
    normed = layer_norm(pair_tensor, norm_in_gain[layer], norm_in_bias[layer]).astype(jnp.bfloat16)
    projected = jnp.dot(normed, proj_weight[layer], preferred_element_type=jnp.float32)
    left_op = (jax.nn.sigmoid(projected[..., 0:width]) * projected[..., width:2 * width]).astype(jnp.bfloat16)
    right_op = (jax.nn.sigmoid(projected[..., 2 * width:3 * width]) * projected[..., 3 * width:4 * width]).astype(jnp.bfloat16)
    gate_values = jax.nn.sigmoid(jnp.dot(normed, gate_weight[layer], preferred_element_type=jnp.float32))
    left_wide = left_op.astype(jnp.float32)
    right_wide = right_op.astype(jnp.float32)
    if layer == 0:
        product = jnp.einsum('ikc,jkc->ijc', left_wide, right_wide)
    else:
        product = jnp.einsum('kic,kjc->ijc', left_wide, right_wide)
    normed_product = layer_norm(product, norm_out_gain[layer], norm_out_bias[layer]).astype(jnp.bfloat16)
    update = gate_values * jnp.dot(normed_product, out_weight[layer], preferred_element_type=jnp.float32)
    return pair_tensor + update

def reference(pair_tensor, norm_in_gain, norm_in_bias, proj_weight, gate_weight, norm_out_gain, norm_out_bias, out_weight):
    current = pair_tensor
    for layer in range(2):
        current = triangle(current, layer, norm_in_gain, norm_in_bias, proj_weight, gate_weight, norm_out_gain, norm_out_bias, out_weight)
    return current
```

```python
import functools

import jax
import jax.numpy as jnp
from jax import lax
from jax.experimental import pallas as pl
from jax.experimental.pallas import tpu as pltpu
from jax.sharding import Mesh, PartitionSpec as P

C = 128
EPS = 1e-05
VMEM_LIMIT = 48 * 1024 * 1024


def full(memory_space=pltpu.VMEM):
    return pl.BlockSpec(memory_space=memory_space)


def params():
    return pltpu.CompilerParams(vmem_limit_bytes=VMEM_LIMIT)


def norm_rows(x, gain_row, bias_row):
    centered = x - jnp.mean(x, axis=-1, keepdims=True)
    variance = jnp.mean(centered * centered, axis=-1, keepdims=True)
    return centered * lax.rsqrt(variance + EPS) * gain_row + bias_row


def dot(a, b, contract):
    return lax.dot_general(a, b, (contract, ((), ())), preferred_element_type=jnp.float32)


def emit_operands(layer, z, s, gain_in, bias_in, proj, gate_w, wide, gate_out):
    rows = z.reshape(256, C)
    normed = norm_rows(rows, gain_in[layer : layer + 1, :], bias_in[layer : layer + 1, :])
    normed = normed.astype(jnp.bfloat16)
    gate_out[s : s + 2] = jax.nn.sigmoid(dot(normed, gate_w[layer], ((1,), (0,)))).reshape(2, 128, C)
    projected = dot(proj[layer], normed, ((0,), (1,)))
    left = jax.nn.sigmoid(projected[0:C]) * projected[C : 2 * C]
    right = jax.nn.sigmoid(projected[2 * C : 3 * C]) * projected[3 * C : 4 * C]
    for t in range(2):
        wide[:, s + t, :] = left[:, 128 * t : 128 * t + 128]
        wide[:, 8 + s + t, :] = right[:, 128 * t : 128 * t + 128]


def first_kernel(z_ref, gain_in, bias_in, proj, gate_w, ops_ref, gate_ref, wide):
    for s in range(0, 8, 2):
        z = jnp.stack([z_ref[:, s], z_ref[:, s + 1]])
        emit_operands(0, z, s, gain_in, bias_in, proj, gate_w, wide, gate_ref)
    ops_ref[...] = wide[...].astype(jnp.bfloat16)


def finish_kernel(layer, y_ref, z_ref, gate_ref, gain_out, bias_out, out_w, *rest):
    if layer == 0:
        gain_in, bias_in, proj, gate_w, z_out, ops_ref, gate_out, y32, wide = rest
    else:
        z_out, y32 = rest
    y = y_ref[...].astype(jnp.float32)
    y32[...] = y
    average = jnp.mean(y, axis=0)
    centered = y - average[None]
    scale = lax.rsqrt(jnp.mean(centered * centered, axis=0) + EPS)
    gain = jnp.transpose(jnp.broadcast_to(gain_out[layer : layer + 1, :], (C, C)))
    bias = jnp.transpose(jnp.broadcast_to(bias_out[layer : layer + 1, :], (C, C)))
    weight = out_w[layer]
    for s in range(0, 8, 2):
        new = []
        for t in (s, s + 1):
            tile = y32[:, t, :]
            normed = (tile - average[t : t + 1]) * scale[t : t + 1] * gain + bias
            update = gate_ref[t] * dot(normed.astype(jnp.bfloat16), weight, ((0,), (0,)))
            value = z_ref[:, t] + update.reshape(4, 32, C)
            z_out[:, t] = value
            new.append(value)
        if layer == 0:
            emit_operands(1, jnp.stack(new), s, gain_in, bias_in, proj, gate_w, wide, gate_out)
    if layer == 0:
        ops_ref[...] = wide[...].astype(jnp.bfloat16)


def swap_groups(tiles):
    lane = lax.broadcasted_iota(jnp.int32, tiles[0].shape, 1)
    low = lane < 64
    even = (lane // 32) % 2 == 0
    t0, t1, t2, t3 = tiles
    u0 = jnp.where(low, t0, pltpu.roll(t2, 64, 1))
    u2 = jnp.where(low, pltpu.roll(t0, 64, 1), t2)
    u1 = jnp.where(low, t1, pltpu.roll(t3, 64, 1))
    u3 = jnp.where(low, pltpu.roll(t1, 64, 1), t3)
    v0 = jnp.where(even, u0, pltpu.roll(u1, 32, 1))
    v1 = jnp.where(even, pltpu.roll(u0, 96, 1), u1)
    v2 = jnp.where(even, u2, pltpu.roll(u3, 32, 1))
    v3 = jnp.where(even, pltpu.roll(u2, 96, 1), u3)
    return v0, v1, v2, v3


def write_back(product, b, y_ref):
    for d, tile in enumerate(swap_groups(product)):
        y_ref[:, 4 * b + d] = tile.reshape(8, 8, 128).astype(jnp.bfloat16)


def tile_of(ref, part, index):
    return ref[:, index, 8 * part : 8 * part + 8, :].astype(jnp.float32).reshape(64, 128)


def outgoing_kernel(core_ref, own, other, y_ref, left, right):
    core = core_ref[0]
    for b in range(4):
        lanes = slice(128 * b, 128 * b + 128)
        cols = range(4 * b, 4 * b + 4)
        for a, tile in enumerate(swap_groups([tile_of(own, 0, q) for q in cols])):
            left[64 * a : 64 * a + 64, lanes] = tile.astype(jnp.bfloat16)
        for ref, place in ((own, core), (other, 1 - core)):
            part = 1 if ref is own else 0
            for a, tile in enumerate(swap_groups([tile_of(ref, part, q) for q in cols])):
                right[:, place, 8 * a : 8 * a + 8, lanes] = tile.reshape(8, 8, 128)
    rows = right[...].reshape(512, 512).astype(jnp.bfloat16)
    product = dot(left[...], rows, ((1,), (1,)))
    for b in range(4):
        write_back([product[64 * a : 64 * a + 64, 128 * b : 128 * b + 128] for a in range(4)], b, y_ref)


def incoming_kernel(core_ref, own, other, y_ref, left, right):
    core = core_ref[0]
    for half, ref in enumerate((own, other)):
        for b in range(4):
            lanes = slice(128 * b, 128 * b + 128)
            for a, tile in enumerate(swap_groups([tile_of(ref, 1, q) for q in range(4 * b, 4 * b + 4)])):
                at = 256 * half + 64 * a
                right[at : at + 64, lanes] = tile.astype(jnp.bfloat16)
        for b in range(2):
            lanes = slice(128 * b, 128 * b + 128)
            picks = [tile_of(ref, 0, 2 * t + core) for t in range(4 * b, 4 * b + 4)]
            for a, tile in enumerate(swap_groups(picks)):
                at = 256 * half + 64 * a
                left[at : at + 64, lanes] = tile.astype(jnp.bfloat16)
    product = dot(left[...], right[...], ((0,), (0,)))
    product = product.reshape(8, 4, 8, 512)
    for b in range(4):
        parts = [product[:, a, :, 128 * b : 128 * b + 128].reshape(64, 128) for a in range(4)]
        write_back(parts, b, y_ref)


def triangle(kernel, core, own, other, left_shape, right_scratch):
    return pl.pallas_call(
        kernel,
        out_shape=jax.ShapeDtypeStruct((8, 16, 8, 128), jnp.bfloat16),
        in_specs=[full(pltpu.SMEM), full(), full()],
        out_specs=full(),
        scratch_shapes=[pltpu.VMEM(left_shape, jnp.bfloat16), right_scratch],
        compiler_params=params(),
    )(core, own, other)


def local(z, gain_in, bias_in, proj, gate_w, gain_out, bias_out, out_w):
    core = lax.axis_index("core").astype(jnp.int32).reshape(1)
    swap = ((0, 1), (1, 0))
    group = ("rh", "col")
    z4 = z.reshape(4, 8, 32, C)
    ops_shape = jax.ShapeDtypeStruct((C, 16, 128), jnp.bfloat16)
    gate_shape = jax.ShapeDtypeStruct((8, 128, C), jnp.float32)
    z_shape = jax.ShapeDtypeStruct((4, 8, 32, C), jnp.float32)
    wide = pltpu.VMEM((C, 16, 128), jnp.float32)
    y32 = pltpu.VMEM((C, 8, 128), jnp.float32)

    ops, gate = pl.pallas_call(
        first_kernel,
        out_shape=(ops_shape, gate_shape),
        in_specs=[full()] * 5,
        out_specs=(full(), full()),
        scratch_shapes=[wide],
        compiler_params=params(),
    )(z4, gain_in, bias_in, proj, gate_w)

    own = lax.all_to_all(ops, group, 0, 0, tiled=True).reshape(8, 16, 16, 128)
    other = lax.ppermute(own[:, :, 8:], "core", swap)
    y = triangle(outgoing_kernel, core, own, other, (256, 512), pltpu.VMEM((8, 2, 32, 512), jnp.float32))
    y = lax.all_to_all(y.reshape(C, 8, 128), group, 0, 0, tiled=True)

    z4, ops, gate = pl.pallas_call(
        functools.partial(finish_kernel, 0),
        out_shape=(z_shape, ops_shape, gate_shape),
        in_specs=[full()] * 10,
        out_specs=(full(), full(), full()),
        scratch_shapes=[y32, wide],
        compiler_params=params(),
    )(y, z4, gate, gain_out, bias_out, out_w, gain_in, bias_in, proj, gate_w)

    own = lax.all_to_all(ops, group, 0, 0, tiled=True).reshape(8, 16, 16, 128)
    other = lax.ppermute(own, "core", swap)
    y = triangle(incoming_kernel, core, own, other, (512, 256), pltpu.VMEM((512, 512), jnp.bfloat16))
    y = lax.all_to_all(y.reshape(C, 8, 128), group, 0, 0, tiled=True)

    out = pl.pallas_call(
        functools.partial(finish_kernel, 1),
        out_shape=z_shape,
        in_specs=[full()] * 6,
        out_specs=full(),
        scratch_shapes=[y32],
        compiler_params=params(),
    )(y, z4, gate, gain_out, bias_out, out_w)
    return out.reshape(32, 32, C)


def solution(mesh):
    fine = Mesh(mesh.devices.reshape(8, 2, 16), ("rh", "core", "col"))
    block = P(("rh", "core"), "col", None)
    return jax.shard_map(
        local,
        mesh=fine,
        in_specs=(block, P(), P(), P(), P(), P(), P(), P()),
        out_specs=block,
        check_vma=False,
    )
```

```python
import functools

import jax
import jax.numpy as jnp
from jax import lax
from jax.experimental import pallas as pl
from jax.experimental.pallas import tpu as pltpu
from jax.sharding import Mesh, PartitionSpec as P

C = 128
EPS = 1e-05
VMEM_LIMIT = 48 * 1024 * 1024


def full(memory_space=pltpu.VMEM):
    return pl.BlockSpec(memory_space=memory_space)


def params():
    return pltpu.CompilerParams(vmem_limit_bytes=VMEM_LIMIT)


def norm_rows(x, gain_row, bias_row):
    centered = x - jnp.mean(x, axis=-1, keepdims=True)
    variance = jnp.mean(centered * centered, axis=-1, keepdims=True)
    return centered * lax.rsqrt(variance + EPS) * gain_row + bias_row


def dot(a, b, contract):
    return lax.dot_general(a, b, (contract, ((), ())), preferred_element_type=jnp.float32)


def emit_operands(z, s, gain_row, bias_row, proj, gate_w, wide, gate_out):
    rows = z.reshape(256, C)
    normed = norm_rows(rows, gain_row, bias_row).astype(jnp.bfloat16)
    gate_out[s : s + 2] = jax.nn.sigmoid(dot(normed, gate_w, ((1,), (0,)))).reshape(2, 128, C)
    projected = dot(proj, normed, ((0,), (1,)))
    left = jax.nn.sigmoid(projected[0:C]) * projected[C : 2 * C]
    right = jax.nn.sigmoid(projected[2 * C : 3 * C]) * projected[3 * C : 4 * C]
    for t in range(2):
        wide[:, s + t, :] = left[:, 128 * t : 128 * t + 128]
        wide[:, 8 + s + t, :] = right[:, 128 * t : 128 * t + 128]


def first_kernel(
    z_hbm, gain_in, bias_in, proj_hbm, gate_hbm, gain_out, bias_out,
    ops_ref, gate_ref, vec_ref, z, proj, gate_w, wide, sems,
):
    vectors = (gain_in, bias_in, gain_out, bias_out)
    pairs = [(ref, vec_ref.at[2 * i : 2 * i + 2]) for i, ref in enumerate(vectors)]
    pairs += [(proj_hbm.at[0], proj), (gate_hbm.at[0], gate_w)]
    early = len(pairs)
    pairs += [(z_hbm.at[:, s : s + 2], z.at[:, s : s + 2]) for s in range(0, 8, 2)]
    order = [0, 1, early, 4, 5, early + 1, early + 2, early + 3, 2, 3]
    copies = [pltpu.make_async_copy(src, dst, sems.at[i]) for i, (src, dst) in enumerate(pairs)]
    for i in order:
        copies[i].start()
    for i in (0, 1, 4, 5):
        copies[i].wait()
    for s in range(0, 8, 2):
        copies[early + s // 2].wait()
        rows = jnp.stack([z[:, s], z[:, s + 1]])
        emit_operands(rows, s, vec_ref[0:1], vec_ref[2:3], proj[...], gate_w[...], wide, gate_ref)
    for i in (2, 3):
        copies[i].wait()
    ops_ref[...] = wide[...].astype(jnp.bfloat16)


def finish_kernel(layer, y_ref, z_ref, gate_ref, vec, out_w, *rest):
    if layer == 0:
        proj, gate_w, z_out, ops_ref, gate_out, y32, wide = rest
    else:
        z_out, y32 = rest
    y = y_ref[...].astype(jnp.float32)
    y32[...] = y
    average = jnp.mean(y, axis=0)
    centered = y - average[None]
    scale = lax.rsqrt(jnp.mean(centered * centered, axis=0) + EPS)
    gain = jnp.transpose(jnp.broadcast_to(vec[4 + layer : 5 + layer, :], (C, C)))
    bias = jnp.transpose(jnp.broadcast_to(vec[6 + layer : 7 + layer, :], (C, C)))
    weight = out_w[layer]
    for s in range(0, 8, 2):
        new = []
        for t in (s, s + 1):
            tile = y32[:, t, :]
            normed = (tile - average[t : t + 1]) * scale[t : t + 1] * gain + bias
            update = gate_ref[t] * dot(normed.astype(jnp.bfloat16), weight, ((0,), (0,)))
            value = z_ref[:, t] + update.reshape(4, 32, C)
            z_out[:, t] = value
            new.append(value)
        if layer == 0:
            emit_operands(jnp.stack(new), s, vec[1:2], vec[3:4], proj[1], gate_w[1], wide, gate_out)
    if layer == 0:
        ops_ref[...] = wide[...].astype(jnp.bfloat16)


def swap_groups(tiles):
    lane = lax.broadcasted_iota(jnp.int32, tiles[0].shape, 1)
    low = lane < 64
    even = (lane // 32) % 2 == 0
    t0, t1, t2, t3 = tiles
    u0 = jnp.where(low, t0, pltpu.roll(t2, 64, 1))
    u2 = jnp.where(low, pltpu.roll(t0, 64, 1), t2)
    u1 = jnp.where(low, t1, pltpu.roll(t3, 64, 1))
    u3 = jnp.where(low, pltpu.roll(t1, 64, 1), t3)
    v0 = jnp.where(even, u0, pltpu.roll(u1, 32, 1))
    v1 = jnp.where(even, pltpu.roll(u0, 96, 1), u1)
    v2 = jnp.where(even, u2, pltpu.roll(u3, 32, 1))
    v3 = jnp.where(even, pltpu.roll(u2, 96, 1), u3)
    return v0, v1, v2, v3


def write_back(product, b, y_ref):
    for d, tile in enumerate(swap_groups(product)):
        y_ref[4 * b + d] = tile.reshape(8, 8, 128).astype(jnp.bfloat16)


def both_of(ref, col):
    both = ref[col].astype(jnp.float32)
    return both[:, 0:8].reshape(64, 128), both[:, 8:16].reshape(64, 128)


def outgoing_half(left, tiles, right, put):
    for b in range(4):
        for a, tile in enumerate(swap_groups(tiles[4 * b : 4 * b + 4])):
            right[:, 8 * a : 8 * a + 8, 128 * b : 128 * b + 128] = tile.reshape(8, 8, 128)
    rows = right[...].reshape(256, 512).astype(jnp.bfloat16)
    product = dot(left[...], rows, ((1,), (1,)))
    for b in range(2):
        parts = [product[64 * a : 64 * a + 64, 128 * b : 128 * b + 128] for a in range(4)]
        for d, tile in enumerate(swap_groups(parts)):
            put(4 * b + d, tile.reshape(8, 8, 128).astype(jnp.bfloat16))


def outgoing_own(own, left, y_half, right):
    tiles = [both_of(own, q) for q in range(16)]
    for b in range(4):
        for a, tile in enumerate(swap_groups([t[0] for t in tiles[4 * b : 4 * b + 4]])):
            left[64 * a : 64 * a + 64, 128 * b : 128 * b + 128] = tile.astype(jnp.bfloat16)

    def put(rh, tile):
        y_half[rh] = tile

    outgoing_half(left, [t[1] for t in tiles], right, put)


def outgoing_other(core_ref, other, left, y_half, y_ref, right):
    core = core_ref[0]
    y_ref[:, core] = y_half[...]

    def put(rh, tile):
        y_ref[rh, 1 - core] = tile

    outgoing_half(left, [other[q].astype(jnp.float32).reshape(64, 128) for q in range(16)], right, put)


def incoming_half(core, ref, left, right):
    for b in range(4):
        lanes = slice(128 * b, 128 * b + 128)
        for a, tile in enumerate(swap_groups([both_of(ref, q)[1] for q in range(4 * b, 4 * b + 4)])):
            right[64 * a : 64 * a + 64, lanes] = tile.astype(jnp.bfloat16)
    for b in range(2):
        lanes = slice(128 * b, 128 * b + 128)
        picks = [both_of(ref, 2 * t + core)[0] for t in range(4 * b, 4 * b + 4)]
        for a, tile in enumerate(swap_groups(picks)):
            left[64 * a : 64 * a + 64, lanes] = tile.astype(jnp.bfloat16)
    return dot(left[...], right[...], ((0,), (0,)))


def incoming_own(core_ref, own, partial, left, right):
    partial[...] = incoming_half(core_ref[0], own, left, right)


def incoming_other(core_ref, other, partial, y_ref, left, right):
    product = partial[...] + incoming_half(core_ref[0], other, left, right)
    product = product.reshape(8, 4, 8, 512)
    for b in range(4):
        parts = [product[:, a, :, 128 * b : 128 * b + 128].reshape(64, 128) for a in range(4)]
        write_back(parts, b, y_ref)


def call(kernel, inputs, outputs, scratch, flops):
    smem = [full(pltpu.SMEM) if v.shape == (1,) else full() for v in inputs]
    return pl.pallas_call(
        kernel,
        out_shape=outputs,
        in_specs=smem,
        out_specs=jax.tree.map(lambda _: full(), outputs),
        scratch_shapes=scratch,
        compiler_params=params(),
        cost_estimate=pl.CostEstimate(flops=flops, bytes_accessed=2 << 20, transcendentals=0),
    )(*inputs)


def local(z, gain_in, bias_in, proj, gate_w, gain_out, bias_out, out_w):
    core = lax.axis_index("core").astype(jnp.int32).reshape(1)
    swap = ((0, 1), (1, 0))
    group = ("yh", "z", "yl", "x")
    z4 = z.reshape(4, 8, 32, C)
    shape = jax.ShapeDtypeStruct
    ops_shape = jax.ShapeDtypeStruct((C, 16, 128), jnp.bfloat16)
    gate_shape = jax.ShapeDtypeStruct((8, 128, C), jnp.float32)
    z_shape = jax.ShapeDtypeStruct((4, 8, 32, C), jnp.float32)
    wide = pltpu.VMEM((C, 16, 128), jnp.float32)
    y32 = pltpu.VMEM((C, 8, 128), jnp.float32)

    ops, gate, vec = pl.pallas_call(
        first_kernel,
        out_shape=(ops_shape, gate_shape, jax.ShapeDtypeStruct((8, C), jnp.float32)),
        in_specs=[full(pltpu.HBM)] * 7,
        out_specs=(full(), full(), full()),
        scratch_shapes=[
            pltpu.VMEM((4, 8, 32, C), jnp.float32),
            pltpu.VMEM((C, 4 * C), jnp.bfloat16),
            pltpu.VMEM((C, C), jnp.bfloat16),
            wide,
            pltpu.SemaphoreType.DMA((10,)),
        ],
        compiler_params=params(),
    )(*[pltpu.with_memory_space_constraint(v, pltpu.HBM) for v in (z4, gain_in, bias_in, proj, gate_w, gain_out, bias_out)])

    own = lax.all_to_all(ops, group, 0, 0, tiled=True).reshape(16, 8, 16, 128)
    other = lax.ppermute(own[:, :, 8:], "core", swap)
    half = 2 * 256 * 256 * 512
    rows = [pltpu.VMEM((8, 32, 512), jnp.float32)]
    outputs = (shape((256, 512), jnp.bfloat16), shape((8, 8, 8, 128), jnp.bfloat16))
    left, y_half = call(outgoing_own, (own,), outputs, rows, half)
    outputs = shape((8, 2, 8, 8, 128), jnp.bfloat16)
    y = call(outgoing_other, (core, other, left, y_half), outputs, rows, half)
    y = lax.all_to_all(y.reshape(C, 8, 128), group, 0, 0, tiled=True)

    z4, ops, gate = pl.pallas_call(
        functools.partial(finish_kernel, 0),
        out_shape=(z_shape, ops_shape, gate_shape),
        in_specs=[full()] * 7,
        out_specs=(full(), full(), full()),
        scratch_shapes=[y32, wide],
        compiler_params=params(),
    )(y, z4, gate, vec, out_w, proj, gate_w)

    own = lax.all_to_all(ops, group, 0, 0, tiled=True).reshape(16, 8, 16, 128)
    other = lax.ppermute(own, "core", swap)
    sides = [pltpu.VMEM((256, 256), jnp.bfloat16), pltpu.VMEM((256, 512), jnp.bfloat16)]
    partial = call(incoming_own, (core, own), shape((256, 512), jnp.float32), sides, half)
    y = call(incoming_other, (core, other, partial), shape((16, 8, 8, 128), jnp.bfloat16), sides, half)
    y = lax.all_to_all(y.reshape(C, 8, 128), group, 0, 0, tiled=True)

    out = pl.pallas_call(
        functools.partial(finish_kernel, 1),
        out_shape=z_shape,
        in_specs=[full()] * 5,
        out_specs=full(),
        scratch_shapes=[y32],
        compiler_params=params(),
    )(y, z4, gate, vec, out_w)
    return out.reshape(32, 32, C)


def solution(mesh):
    fine = Mesh(mesh.devices.reshape(2, 4, 2, 2, 8), ("yl", "x", "core", "yh", "z"))
    block = P(("yl", "x", "core"), ("yh", "z"), None)
    return jax.shard_map(
        local,
        mesh=fine,
        in_specs=(block, P(), P(), P(), P(), P(), P(), P()),
        out_specs=block,
        check_vma=False,
    )
```

```python
import functools

import jax
import jax.numpy as jnp
from jax import lax
from jax.experimental import pallas as pl
from jax.experimental.pallas import tpu as pltpu
from jax.sharding import Mesh, PartitionSpec as P

C = 128
EPS = 1e-05
VMEM_LIMIT = 48 * 1024 * 1024


def full(memory_space=pltpu.VMEM):
    return pl.BlockSpec(memory_space=memory_space)


def params():
    return pltpu.CompilerParams(vmem_limit_bytes=VMEM_LIMIT)


def norm_rows(x, gain_row, bias_row):
    centered = x - jnp.mean(x, axis=-1, keepdims=True)
    variance = jnp.mean(centered * centered, axis=-1, keepdims=True)
    return centered * lax.rsqrt(variance + EPS) * gain_row + bias_row


def dot(a, b, contract):
    return lax.dot_general(a, b, (contract, ((), ())), preferred_element_type=jnp.float32)


def emit_operands(z, s, gain_row, bias_row, proj, wide, normed_out):
    rows = z.reshape(256, C)
    normed = norm_rows(rows, gain_row, bias_row).astype(jnp.bfloat16)
    normed_out[s : s + 2] = normed.reshape(2, 128, C)
    projected = dot(proj, normed, ((0,), (1,)))
    left = jax.nn.sigmoid(projected[0:C]) * projected[C : 2 * C]
    right = jax.nn.sigmoid(projected[2 * C : 3 * C]) * projected[3 * C : 4 * C]
    for t in range(2):
        wide[s + t] = left[:, 128 * t : 128 * t + 128].astype(jnp.bfloat16)
        wide[8 + s + t] = right[:, 128 * t : 128 * t + 128].astype(jnp.bfloat16)


def write_gate(normed, gate_w, gate):
    values = dot(normed[...].reshape(1024, C), gate_w, ((1,), (0,)))
    gate[...] = jax.nn.sigmoid(values).reshape(8, 128, C)


def first_kernel(
    z_hbm, gain_in, bias_in, proj_hbm, gate_hbm, gain_out, bias_out,
    ops_ref, normed_ref, vec_ref, gate_w, z, proj, wide, sems,
):
    vectors = (gain_in, bias_in, gain_out, bias_out)
    pairs = [(z_hbm, z), (proj_hbm.at[0], proj)]
    pairs += [(ref, vec_ref.at[2 * i : 2 * i + 2]) for i, ref in enumerate(vectors)]
    pairs += [(gate_hbm, gate_w)]
    copies = [pltpu.make_async_copy(src, dst, sems.at[i]) for i, (src, dst) in enumerate(pairs)]
    for copy in copies:
        copy.start()
    for copy in copies:
        copy.wait()
    for s in range(0, 8, 2):
        rows = jnp.stack([z[:, s], z[:, s + 1]])
        emit_operands(rows, s, vec_ref[0:1], vec_ref[2:3], proj[...], wide, normed_ref)
    ops_ref[...] = jnp.swapaxes(wide[...], 0, 1)


def finish_kernel(layer, y_ref, z_ref, gate_ref, vec, out_w, *rest):
    if layer == 0:
        proj, z_out, ops_ref, normed_out, y32, wide = rest
    else:
        z_hbm, y32, z_out, sems = rest
    y32[...] = jnp.swapaxes(y_ref[...].astype(jnp.float32), 0, 1)
    gain = jnp.transpose(jnp.broadcast_to(vec[4 + layer : 5 + layer, :], (C, C)))
    bias = jnp.transpose(jnp.broadcast_to(vec[6 + layer : 7 + layer, :], (C, C)))
    weight = out_w[layer]
    copies = []
    for s in range(0, 8, 2):
        new = []
        for t in (s, s + 1):
            tile = y32[t]
            centered = tile - jnp.mean(tile, axis=0, keepdims=True)
            scale = lax.rsqrt(jnp.mean(centered * centered, axis=0, keepdims=True) + EPS)
            normed = centered * scale * gain + bias
            update = gate_ref[t] * dot(normed.astype(jnp.bfloat16), weight, ((0,), (0,)))
            value = z_ref[:, t] + update.reshape(4, 32, C)
            z_out[:, t] = value
            new.append(value)
        if layer == 0:
            emit_operands(jnp.stack(new), s, vec[1:2], vec[3:4], proj[1], wide, normed_out)
        elif s % 4 == 2:
            part = slice(s - 2, s + 2)
            copies.append(pltpu.make_async_copy(z_out.at[:, part], z_hbm.at[:, part], sems.at[s // 4]))
            copies[-1].start()
    if layer == 0:
        ops_ref[...] = jnp.swapaxes(wide[...], 0, 1)
    for copy in copies:
        copy.wait()


def swap_groups(tiles):
    lane = lax.broadcasted_iota(jnp.int32, tiles[0].shape, 1)
    low = lane < 64
    even = (lane // 32) % 2 == 0
    t0, t1, t2, t3 = tiles
    u0 = jnp.where(low, t0, pltpu.roll(t2, 64, 1))
    u2 = jnp.where(low, pltpu.roll(t0, 64, 1), t2)
    u1 = jnp.where(low, t1, pltpu.roll(t3, 64, 1))
    u3 = jnp.where(low, pltpu.roll(t1, 64, 1), t3)
    v0 = jnp.where(even, u0, pltpu.roll(u1, 32, 1))
    v1 = jnp.where(even, pltpu.roll(u0, 96, 1), u1)
    v2 = jnp.where(even, u2, pltpu.roll(u3, 32, 1))
    v3 = jnp.where(even, pltpu.roll(u2, 96, 1), u3)
    return v0, v1, v2, v3


def write_back(product, b, y_ref):
    for d, tile in enumerate(swap_groups(product)):
        y_ref[4 * b + d] = tile.reshape(8, 8, 128).astype(jnp.bfloat16)


def both_of(ref, col):
    both = ref[col].astype(jnp.float32)
    return both[:, 0:8].reshape(64, 128), both[:, 8:16].reshape(64, 128)


def outgoing_half(left, tiles, right, put):
    for b in range(4):
        for a, tile in enumerate(swap_groups(tiles[4 * b : 4 * b + 4])):
            right[:, 8 * a : 8 * a + 8, 128 * b : 128 * b + 128] = tile.reshape(8, 8, 128)
    rows = right[...].reshape(256, 512).astype(jnp.bfloat16)
    product = dot(left[...], rows, ((1,), (1,)))
    for b in range(2):
        parts = [product[64 * a : 64 * a + 64, 128 * b : 128 * b + 128] for a in range(4)]
        for d, tile in enumerate(swap_groups(parts)):
            put(4 * b + d, tile.reshape(8, 8, 128).astype(jnp.bfloat16))


def outgoing_own(own, normed, gate_w, left, y_half, gate, right):
    write_gate(normed, gate_w[0], gate)
    tiles = [both_of(own, q) for q in range(16)]
    for b in range(4):
        for a, tile in enumerate(swap_groups([t[0] for t in tiles[4 * b : 4 * b + 4]])):
            left[64 * a : 64 * a + 64, 128 * b : 128 * b + 128] = tile.astype(jnp.bfloat16)

    def put(rh, tile):
        y_half[rh] = tile

    outgoing_half(left, [t[1] for t in tiles], right, put)


def outgoing_other(core_ref, other, left, y_half, y_ref, right):
    core = core_ref[0]
    y_ref[:, core] = y_half[...]

    def put(rh, tile):
        y_ref[rh, 1 - core] = tile

    outgoing_half(left, [other[q].astype(jnp.float32).reshape(64, 128) for q in range(16)], right, put)


def incoming_half(core, ref, left, right):
    for b in range(4):
        lanes = slice(128 * b, 128 * b + 128)
        for a, tile in enumerate(swap_groups([both_of(ref, q)[1] for q in range(4 * b, 4 * b + 4)])):
            right[64 * a : 64 * a + 64, lanes] = tile.astype(jnp.bfloat16)
    for b in range(2):
        lanes = slice(128 * b, 128 * b + 128)
        picks = [both_of(ref, 2 * t + core)[0] for t in range(4 * b, 4 * b + 4)]
        for a, tile in enumerate(swap_groups(picks)):
            left[64 * a : 64 * a + 64, lanes] = tile.astype(jnp.bfloat16)
    return dot(left[...], right[...], ((0,), (0,)))


def incoming_own(core_ref, own, normed, gate_w, partial, gate, left, right):
    write_gate(normed, gate_w[1], gate)
    partial[...] = incoming_half(core_ref[0], own, left, right)


def incoming_other(core_ref, other, partial, y_ref, left, right):
    product = partial[...] + incoming_half(core_ref[0], other, left, right)
    product = product.reshape(8, 4, 8, 512)
    for b in range(4):
        parts = [product[:, a, :, 128 * b : 128 * b + 128].reshape(64, 128) for a in range(4)]
        write_back(parts, b, y_ref)


def call(kernel, inputs, outputs, scratch, flops):
    smem = [full(pltpu.SMEM) if v.shape == (1,) else full() for v in inputs]
    return pl.pallas_call(
        kernel,
        out_shape=outputs,
        in_specs=smem,
        out_specs=jax.tree.map(lambda _: full(), outputs),
        scratch_shapes=scratch,
        compiler_params=params(),
        cost_estimate=pl.CostEstimate(flops=flops, bytes_accessed=2 << 20, transcendentals=0),
    )(*inputs)


def local(z, gain_in, bias_in, proj, gate_w, gain_out, bias_out, out_w):
    core = lax.axis_index("core").astype(jnp.int32).reshape(1)
    swap = ((0, 1), (1, 0))
    group = ("yh", "z", "yl", "x")
    z4 = z.reshape(4, 8, 32, C)
    shape = jax.ShapeDtypeStruct
    ops_shape = jax.ShapeDtypeStruct((C, 16, 128), jnp.bfloat16)
    normed_shape = shape((8, 128, C), jnp.bfloat16)
    gate_shape = jax.ShapeDtypeStruct((8, 128, C), jnp.float32)
    z_shape = jax.ShapeDtypeStruct((4, 8, 32, C), jnp.float32)
    wide = pltpu.VMEM((16, C, 128), jnp.bfloat16)
    y32 = pltpu.VMEM((8, C, 128), jnp.float32)

    operands = [pltpu.with_memory_space_constraint(v, pltpu.HBM) for v in (z4, gain_in, bias_in, proj, gate_w, gain_out, bias_out)]
    ops, normed, vec, gate_w = pl.pallas_call(
        first_kernel,
        out_shape=(ops_shape, normed_shape, shape((8, C), jnp.float32), shape((2, C, C), jnp.bfloat16)),
        in_specs=[full(pltpu.HBM)] * 7,
        out_specs=(full(), full(), full(), full()),
        scratch_shapes=[
            pltpu.VMEM((4, 8, 32, C), jnp.float32),
            pltpu.VMEM((C, 4 * C), jnp.bfloat16),
            wide,
            pltpu.SemaphoreType.DMA((7,)),
        ],
        compiler_params=params(),
    )(*operands)

    own = lax.all_to_all(ops, group, 0, 0, tiled=True).reshape(16, 8, 16, 128)
    other = lax.ppermute(own[:, :, 8:], "core", swap)
    half = 2 * 256 * 256 * 512
    rows = [pltpu.VMEM((8, 32, 512), jnp.float32)]
    outputs = (shape((256, 512), jnp.bfloat16), shape((8, 8, 8, 128), jnp.bfloat16), gate_shape)
    left, y_half, gate = call(outgoing_own, (own, normed, gate_w), outputs, rows, half)
    outputs = shape((8, 2, 8, 8, 128), jnp.bfloat16)
    y = call(outgoing_other, (core, other, left, y_half), outputs, rows, half)
    y = lax.all_to_all(y.reshape(C, 8, 128), group, 0, 0, tiled=True)

    z4, ops, normed = pl.pallas_call(
        functools.partial(finish_kernel, 0),
        out_shape=(z_shape, ops_shape, normed_shape),
        in_specs=[full()] * 6,
        out_specs=(full(), full(), full()),
        scratch_shapes=[y32, wide],
        compiler_params=params(),
    )(y, z4, gate, vec, out_w, proj)

    own = lax.all_to_all(ops, group, 0, 0, tiled=True).reshape(16, 8, 16, 128)
    other = lax.ppermute(own, "core", swap)
    sides = [pltpu.VMEM((256, 256), jnp.bfloat16), pltpu.VMEM((256, 512), jnp.bfloat16)]
    outputs = (shape((256, 512), jnp.float32), gate_shape)
    partial, gate = call(incoming_own, (core, own, normed, gate_w), outputs, sides, half)
    y = call(incoming_other, (core, other, partial), shape((16, 8, 8, 128), jnp.bfloat16), sides, half)
    y = lax.all_to_all(y.reshape(C, 8, 128), group, 0, 0, tiled=True)

    out = pl.pallas_call(
        functools.partial(finish_kernel, 1),
        out_shape=z_shape,
        in_specs=[full()] * 5,
        out_specs=full(pltpu.HBM),
        scratch_shapes=[y32, pltpu.VMEM((4, 8, 32, C), jnp.float32), pltpu.SemaphoreType.DMA((2,))],
        compiler_params=params(),
    )(y, z4, gate, vec, out_w)
    return out.reshape(32, 32, C)


def solution(mesh):
    fine = Mesh(mesh.devices.reshape(2, 4, 2, 2, 8), ("yl", "x", "core", "yh", "z"))
    block = P(("yl", "x", "core"), ("yh", "z"), None)
    return jax.shard_map(
        local,
        mesh=fine,
        in_specs=(block, P(), P(), P(), P(), P(), P(), P()),
        out_specs=block,
        check_vma=False,
    )
```

```python
import functools

import jax
import jax.numpy as jnp
from jax import lax
from jax.experimental import pallas as pl
from jax.experimental.pallas import tpu as pltpu
from jax.sharding import Mesh, PartitionSpec as P

C = 128
EPS = 1e-05
VMEM_LIMIT = 48 * 1024 * 1024


def full(memory_space=pltpu.VMEM):
    return pl.BlockSpec(memory_space=memory_space)


def params():
    return pltpu.CompilerParams(vmem_limit_bytes=VMEM_LIMIT)


def norm_rows(x, gain_row, bias_row):
    centered = x - jnp.mean(x, axis=-1, keepdims=True)
    variance = jnp.mean(centered * centered, axis=-1, keepdims=True)
    return centered * lax.rsqrt(variance + EPS) * gain_row + bias_row


def dot(a, b, contract):
    return lax.dot_general(a, b, (contract, ((), ())), preferred_element_type=jnp.float32)


def emit_operands(z, s, gain_row, bias_row, proj, wide, normed_out):
    rows = z.reshape(256, C)
    normed = norm_rows(rows, gain_row, bias_row).astype(jnp.bfloat16)
    normed_out[s : s + 2] = normed.reshape(2, 128, C)
    projected = dot(proj, normed, ((0,), (1,)))
    left = jax.nn.sigmoid(projected[0:C]) * projected[C : 2 * C]
    right = jax.nn.sigmoid(projected[2 * C : 3 * C]) * projected[3 * C : 4 * C]
    for t in range(2):
        wide[s + t] = left[:, 128 * t : 128 * t + 128].astype(jnp.bfloat16)
        wide[8 + s + t] = right[:, 128 * t : 128 * t + 128].astype(jnp.bfloat16)


def write_gate(normed, gate_w, gate):
    values = dot(normed[...].reshape(1024, C), gate_w, ((1,), (0,)))
    gate[...] = jax.nn.sigmoid(values).reshape(8, 128, C)


def first_kernel(
    z_hbm, gain_in, bias_in, proj_hbm, gate_hbm, gain_out, bias_out,
    ops_ref, normed_ref, vec_ref, gate_w, z, proj, wide, sems,
):
    vectors = (gain_in, bias_in, gain_out, bias_out)
    pairs = [(z_hbm, z), (proj_hbm.at[0], proj)]
    pairs += [(ref, vec_ref.at[2 * i : 2 * i + 2]) for i, ref in enumerate(vectors)]
    pairs += [(gate_hbm, gate_w)]
    copies = [pltpu.make_async_copy(src, dst, sems.at[i]) for i, (src, dst) in enumerate(pairs)]
    for copy in copies:
        copy.start()
    for copy in copies:
        copy.wait()
    for s in range(0, 8, 2):
        rows = jnp.stack([z[:, s], z[:, s + 1]])
        emit_operands(rows, s, vec_ref[0:1], vec_ref[2:3], proj[...], wide, normed_ref)
    ops_ref[...] = jnp.swapaxes(wide[...], 0, 1)


def finish_kernel(layer, y_ref, z_ref, gate_ref, vec, out_w, *rest):
    if layer == 0:
        proj, z_out, ops_ref, normed_out, y32, wide = rest
    else:
        z_hbm, y32, z_out, sems = rest
    y32[...] = jnp.swapaxes(y_ref[...].astype(jnp.float32), 0, 1)
    gain = jnp.transpose(jnp.broadcast_to(vec[4 + layer : 5 + layer, :], (C, C)))
    bias = jnp.transpose(jnp.broadcast_to(vec[6 + layer : 7 + layer, :], (C, C)))
    weight = jnp.concatenate([out_w[layer], out_w[layer]])
    copies = []
    for s in range(0, 8, 2):
        new = []
        for t in (s, s + 1):
            tile = y32[t]
            centered = tile - jnp.mean(tile, axis=0, keepdims=True)
            scale = lax.rsqrt(jnp.mean(centered * centered, axis=0, keepdims=True) + EPS)
            normed = centered * scale * gain + bias
            high = normed.astype(jnp.bfloat16)
            low = (normed - high.astype(jnp.float32)).astype(jnp.bfloat16)
            both = jnp.concatenate([high, low])
            update = gate_ref[t] * dot(both, weight, ((0,), (0,)))
            value = z_ref[:, t] + update.reshape(4, 32, C)
            z_out[:, t] = value
            new.append(value)
        if layer == 0:
            emit_operands(jnp.stack(new), s, vec[1:2], vec[3:4], proj[1], wide, normed_out)
        elif s % 4 == 2:
            part = slice(s - 2, s + 2)
            copies.append(pltpu.make_async_copy(z_out.at[:, part], z_hbm.at[:, part], sems.at[s // 4]))
            copies[-1].start()
    if layer == 0:
        ops_ref[...] = jnp.swapaxes(wide[...], 0, 1)
    for copy in copies:
        copy.wait()


def swap_groups(tiles):
    lane = lax.broadcasted_iota(jnp.int32, tiles[0].shape, 1)
    low = lane < 64
    even = (lane // 32) % 2 == 0
    t0, t1, t2, t3 = tiles
    u0 = jnp.where(low, t0, pltpu.roll(t2, 64, 1))
    u2 = jnp.where(low, pltpu.roll(t0, 64, 1), t2)
    u1 = jnp.where(low, t1, pltpu.roll(t3, 64, 1))
    u3 = jnp.where(low, pltpu.roll(t1, 64, 1), t3)
    v0 = jnp.where(even, u0, pltpu.roll(u1, 32, 1))
    v1 = jnp.where(even, pltpu.roll(u0, 96, 1), u1)
    v2 = jnp.where(even, u2, pltpu.roll(u3, 32, 1))
    v3 = jnp.where(even, pltpu.roll(u2, 96, 1), u3)
    return v0, v1, v2, v3


def write_back(product, b, y_ref):
    for d, tile in enumerate(swap_groups([p.astype(jnp.bfloat16) for p in product])):
        y_ref[4 * b + d] = tile.reshape(8, 8, 128)


def both_of(ref, col):
    both = ref[col].astype(jnp.float32)
    return both[:, 0:8].reshape(64, 128), both[:, 8:16].reshape(64, 128)


def outgoing_half(left, tiles, right, put):
    for b in range(4):
        for a, tile in enumerate(swap_groups(tiles[4 * b : 4 * b + 4])):
            right[:, 8 * a : 8 * a + 8, 128 * b : 128 * b + 128] = tile.reshape(8, 8, 128)
    rows = right[...].reshape(256, 512).astype(jnp.bfloat16)
    product = dot(left[...], rows, ((1,), (1,)))
    for b in range(2):
        parts = [product[64 * a : 64 * a + 64, 128 * b : 128 * b + 128] for a in range(4)]
        for d, tile in enumerate(swap_groups([p.astype(jnp.bfloat16) for p in parts])):
            put(4 * b + d, tile.reshape(8, 8, 128))


def outgoing_own(own, normed, gate_w, left, y_half, gate, right):
    write_gate(normed, gate_w[0], gate)
    tiles = [both_of(own, q) for q in range(16)]
    for b in range(4):
        for a, tile in enumerate(swap_groups([t[0] for t in tiles[4 * b : 4 * b + 4]])):
            left[64 * a : 64 * a + 64, 128 * b : 128 * b + 128] = tile.astype(jnp.bfloat16)

    def put(rh, tile):
        y_half[rh] = tile

    outgoing_half(left, [t[1] for t in tiles], right, put)


def outgoing_other(core_ref, other, left, y_half, y_ref, right):
    core = core_ref[0]
    y_ref[:, core] = y_half[...]

    def put(rh, tile):
        y_ref[rh, 1 - core] = tile

    outgoing_half(left, [other[q].astype(jnp.float32).reshape(64, 128) for q in range(16)], right, put)


def incoming_half(core, ref, left, right):
    for b in range(4):
        lanes = slice(128 * b, 128 * b + 128)
        for a, tile in enumerate(swap_groups([both_of(ref, q)[1] for q in range(4 * b, 4 * b + 4)])):
            right[64 * a : 64 * a + 64, lanes] = tile.astype(jnp.bfloat16)
    for b in range(2):
        lanes = slice(128 * b, 128 * b + 128)
        picks = [both_of(ref, 2 * t + core)[0] for t in range(4 * b, 4 * b + 4)]
        for a, tile in enumerate(swap_groups(picks)):
            left[64 * a : 64 * a + 64, lanes] = tile.astype(jnp.bfloat16)
    return dot(left[...], right[...], ((0,), (0,)))


def incoming_own(core_ref, own, normed, gate_w, partial, gate, left, right):
    write_gate(normed, gate_w[1], gate)
    partial[...] = incoming_half(core_ref[0], own, left, right)


def incoming_other(core_ref, other, partial, y_ref, left, right):
    product = partial[...] + incoming_half(core_ref[0], other, left, right)
    product = product.reshape(8, 4, 8, 512)
    for b in range(4):
        parts = [product[:, a, :, 128 * b : 128 * b + 128].reshape(64, 128) for a in range(4)]
        write_back(parts, b, y_ref)


def call(kernel, inputs, outputs, scratch, flops):
    smem = [full(pltpu.SMEM) if v.shape == (1,) else full() for v in inputs]
    return pl.pallas_call(
        kernel,
        out_shape=outputs,
        in_specs=smem,
        out_specs=jax.tree.map(lambda _: full(), outputs),
        scratch_shapes=scratch,
        compiler_params=params(),
        cost_estimate=pl.CostEstimate(flops=flops, bytes_accessed=2 << 20, transcendentals=0),
    )(*inputs)


def local(z, gain_in, bias_in, proj, gate_w, gain_out, bias_out, out_w):
    core = lax.axis_index("core").astype(jnp.int32).reshape(1)
    swap = ((0, 1), (1, 0))
    group = ("yh", "z", "yl", "x")
    z4 = z.reshape(4, 8, 32, C)
    shape = jax.ShapeDtypeStruct
    ops_shape = jax.ShapeDtypeStruct((C, 16, 128), jnp.bfloat16)
    normed_shape = shape((8, 128, C), jnp.bfloat16)
    gate_shape = jax.ShapeDtypeStruct((8, 128, C), jnp.float32)
    z_shape = jax.ShapeDtypeStruct((4, 8, 32, C), jnp.float32)
    wide = pltpu.VMEM((16, C, 128), jnp.bfloat16)
    y32 = pltpu.VMEM((8, C, 128), jnp.float32)

    operands = [pltpu.with_memory_space_constraint(v, pltpu.HBM) for v in (z4, gain_in, bias_in, proj, gate_w, gain_out, bias_out)]
    ops, normed, vec, gate_w = pl.pallas_call(
        first_kernel,
        out_shape=(ops_shape, normed_shape, shape((8, C), jnp.float32), shape((2, C, C), jnp.bfloat16)),
        in_specs=[full(pltpu.HBM)] * 7,
        out_specs=(full(), full(), full(), full()),
        scratch_shapes=[
            pltpu.VMEM((4, 8, 32, C), jnp.float32),
            pltpu.VMEM((C, 4 * C), jnp.bfloat16),
            wide,
            pltpu.SemaphoreType.DMA((7,)),
        ],
        compiler_params=params(),
    )(*operands)

    own = lax.all_to_all(ops, group, 0, 0, tiled=True).reshape(16, 8, 16, 128)
    other = lax.ppermute(own[:, :, 8:], "core", swap)
    half = 2 * 256 * 256 * 512
    rows = [pltpu.VMEM((8, 32, 512), jnp.float32)]
    outputs = (shape((256, 512), jnp.bfloat16), shape((8, 8, 8, 128), jnp.bfloat16), gate_shape)
    left, y_half, gate = call(outgoing_own, (own, normed, gate_w), outputs, rows, half)
    outputs = shape((8, 2, 8, 8, 128), jnp.bfloat16)
    y = call(outgoing_other, (core, other, left, y_half), outputs, rows, half)
    y = lax.all_to_all(y.reshape(C, 8, 128), group, 0, 0, tiled=True)

    z4, ops, normed = pl.pallas_call(
        functools.partial(finish_kernel, 0),
        out_shape=(z_shape, ops_shape, normed_shape),
        in_specs=[full()] * 6,
        out_specs=(full(), full(), full()),
        scratch_shapes=[y32, wide],
        compiler_params=params(),
    )(y, z4, gate, vec, out_w, proj)

    own = lax.all_to_all(ops, group, 0, 0, tiled=True).reshape(16, 8, 16, 128)
    other = lax.ppermute(own, "core", swap)
    sides = [pltpu.VMEM((256, 256), jnp.bfloat16), pltpu.VMEM((256, 512), jnp.bfloat16)]
    outputs = (shape((256, 512), jnp.float32), gate_shape)
    partial, gate = call(incoming_own, (core, own, normed, gate_w), outputs, sides, half)
    y = call(incoming_other, (core, other, partial), shape((16, 8, 8, 128), jnp.bfloat16), sides, half)
    y = lax.all_to_all(y.reshape(C, 8, 128), group, 0, 0, tiled=True)

    out = pl.pallas_call(
        functools.partial(finish_kernel, 1),
        out_shape=z_shape,
        in_specs=[full()] * 5,
        out_specs=full(pltpu.HBM),
        scratch_shapes=[y32, pltpu.VMEM((4, 8, 32, C), jnp.float32), pltpu.SemaphoreType.DMA((2,))],
        compiler_params=params(),
    )(y, z4, gate, vec, out_w)
    return out.reshape(32, 32, C)


def solution(mesh):
    fine = Mesh(mesh.devices.reshape(2, 4, 2, 2, 8), ("yl", "x", "core", "yh", "z"))
    block = P(("yl", "x", "core"), ("yh", "z"), None)
    return jax.shard_map(
        local,
        mesh=fine,
        in_specs=(block, P(), P(), P(), P(), P(), P(), P()),
        out_specs=block,
        check_vma=False,
    )
```

```python
import functools

import jax
import jax.numpy as jnp
from jax import lax
from jax.experimental import pallas as pl
from jax.experimental.pallas import tpu as pltpu
from jax.sharding import Mesh, PartitionSpec as P

RH_ORDER = (6, 2, 7, 0, 4, 5, 1, 3)
COL_ORDER = (7, 11, 13, 9, 2, 0, 3, 4, 10, 1, 15, 8, 6, 5, 12, 14)
RANKS = [8 * col + rh for rh in RH_ORDER for col in COL_ORDER]
C = 128
EPS = 1e-05
VMEM_LIMIT = 48 * 1024 * 1024


def full(memory_space=pltpu.VMEM):
    return pl.BlockSpec(memory_space=memory_space)


def params():
    return pltpu.CompilerParams(vmem_limit_bytes=VMEM_LIMIT)


def norm_rows(x, gain_row, bias_row):
    centered = x - jnp.mean(x, axis=-1, keepdims=True)
    variance = jnp.mean(centered * centered, axis=-1, keepdims=True)
    return centered * lax.rsqrt(variance + EPS) * gain_row + bias_row


def dot(a, b, contract):
    return lax.dot_general(a, b, (contract, ((), ())), preferred_element_type=jnp.float32)


def emit_operands(z, s, gain_row, bias_row, proj, wide, normed_out):
    rows = z.reshape(256, C)
    normed = norm_rows(rows, gain_row, bias_row).astype(jnp.bfloat16)
    normed_out[s : s + 2] = normed.reshape(2, 128, C)
    projected = dot(proj, normed, ((0,), (1,)))
    left = jax.nn.sigmoid(projected[0:C]) * projected[C : 2 * C]
    right = jax.nn.sigmoid(projected[2 * C : 3 * C]) * projected[3 * C : 4 * C]
    for t in range(2):
        wide[s + t] = left[:, 128 * t : 128 * t + 128].astype(jnp.bfloat16)
        wide[8 + s + t] = right[:, 128 * t : 128 * t + 128].astype(jnp.bfloat16)


def write_gate(normed, gate_w, gate):
    values = dot(normed[...].reshape(1024, C), gate_w, ((1,), (0,)))
    gate[...] = jax.nn.sigmoid(values).reshape(8, 128, C)


def first_kernel(
    z_hbm, gain_in, bias_in, proj_hbm, gate_hbm, gain_out, bias_out,
    ops_ref, normed_ref, vec_ref, gate_w, z, proj, wide, sems,
):
    vectors = (gain_in, bias_in, gain_out, bias_out)
    pairs = [(z_hbm, z), (proj_hbm.at[0], proj)]
    pairs += [(ref, vec_ref.at[2 * i : 2 * i + 2]) for i, ref in enumerate(vectors)]
    pairs += [(gate_hbm, gate_w)]
    copies = [pltpu.make_async_copy(src, dst, sems.at[i]) for i, (src, dst) in enumerate(pairs)]
    for copy in copies:
        copy.start()
    for copy in copies:
        copy.wait()
    for s in range(0, 8, 2):
        rows = jnp.stack([z[:, s], z[:, s + 1]])
        emit_operands(rows, s, vec_ref[0:1], vec_ref[2:3], proj[...], wide, normed_ref)
    ops_ref[...] = jnp.swapaxes(wide[...], 0, 1)


def finish_kernel(layer, y_ref, z_ref, gate_ref, vec, out_w, *rest):
    if layer == 0:
        proj, z_out, ops_ref, normed_out, y32, wide = rest
    else:
        z_hbm, y32, z_out, sems = rest
    y32[...] = jnp.swapaxes(y_ref[...].astype(jnp.float32), 0, 1)
    gain = jnp.transpose(jnp.broadcast_to(vec[4 + layer : 5 + layer, :], (C, C)))
    bias = jnp.transpose(jnp.broadcast_to(vec[6 + layer : 7 + layer, :], (C, C)))
    weight = jnp.concatenate([out_w[layer], out_w[layer]])
    copies = []
    for s in range(0, 8, 2):
        new = []
        for t in (s, s + 1):
            tile = y32[t]
            centered = tile - jnp.mean(tile, axis=0, keepdims=True)
            scale = lax.rsqrt(jnp.mean(centered * centered, axis=0, keepdims=True) + EPS)
            normed = centered * scale * gain + bias
            high = normed.astype(jnp.bfloat16)
            low = (normed - high.astype(jnp.float32)).astype(jnp.bfloat16)
            both = jnp.concatenate([high, low])
            update = gate_ref[t] * dot(both, weight, ((0,), (0,)))
            value = z_ref[:, t] + update.reshape(4, 32, C)
            z_out[:, t] = value
            new.append(value)
        if layer == 0:
            emit_operands(jnp.stack(new), s, vec[1:2], vec[3:4], proj[1], wide, normed_out)
        elif s % 4 == 2:
            part = slice(s - 2, s + 2)
            copies.append(pltpu.make_async_copy(z_out.at[:, part], z_hbm.at[:, part], sems.at[s // 4]))
            copies[-1].start()
    if layer == 0:
        ops_ref[...] = jnp.swapaxes(wide[...], 0, 1)
    for copy in copies:
        copy.wait()


def swap_groups(tiles):
    lane = lax.broadcasted_iota(jnp.int32, tiles[0].shape, 1)
    low = lane < 64
    even = (lane // 32) % 2 == 0
    t0, t1, t2, t3 = tiles
    u0 = jnp.where(low, t0, pltpu.roll(t2, 64, 1))
    u2 = jnp.where(low, pltpu.roll(t0, 64, 1), t2)
    u1 = jnp.where(low, t1, pltpu.roll(t3, 64, 1))
    u3 = jnp.where(low, pltpu.roll(t1, 64, 1), t3)
    v0 = jnp.where(even, u0, pltpu.roll(u1, 32, 1))
    v1 = jnp.where(even, pltpu.roll(u0, 96, 1), u1)
    v2 = jnp.where(even, u2, pltpu.roll(u3, 32, 1))
    v3 = jnp.where(even, pltpu.roll(u2, 96, 1), u3)
    return v0, v1, v2, v3


def write_back(product, b, y_ref):
    for d, tile in enumerate(swap_groups([p.astype(jnp.bfloat16) for p in product])):
        y_ref[:, COL_ORDER.index(4 * b + d)] = tile.reshape(8, 8, 128)


def place(m, parity):
    even, odd = (COL_ORDER.index(2 * RH_ORDER[m] + i) for i in range(2))
    return even + parity * (odd - even)


def both_of(ref, n):
    both = ref[:, n].astype(jnp.float32)
    return both[:, 0:8].reshape(64, 128), both[:, 8:16].reshape(64, 128)


def outgoing_half(left, tiles, right, put):
    for b in range(4):
        for a, tile in enumerate(swap_groups(tiles[4 * b : 4 * b + 4])):
            right[:, 8 * a : 8 * a + 8, 128 * b : 128 * b + 128] = tile.reshape(8, 8, 128)
    rows = right[...].reshape(256, 512).astype(jnp.bfloat16)
    product = dot(left[...], rows, ((1,), (1,)))
    for b in range(2):
        parts = [product[64 * a : 64 * a + 64, 128 * b : 128 * b + 128] for a in range(4)]
        for d, tile in enumerate(swap_groups([p.astype(jnp.bfloat16) for p in parts])):
            put(4 * b + d, tile.reshape(8, 8, 128))


def outgoing_own(own, normed, gate_w, left, y_half, gate, right):
    write_gate(normed, gate_w[0], gate)
    tiles = [both_of(own, COL_ORDER.index(q)) for q in range(16)]
    for b in range(4):
        for a, tile in enumerate(swap_groups([t[0] for t in tiles[4 * b : 4 * b + 4]])):
            left[64 * a : 64 * a + 64, 128 * b : 128 * b + 128] = tile.astype(jnp.bfloat16)

    def put(m, tile):
        y_half[m] = tile

    outgoing_half(left, [t[1] for t in tiles], right, put)


def outgoing_other(core_ref, other, left, y_half, y_ref, right):
    core = core_ref[0]
    for m in range(8):
        y_ref[:, place(m, core)] = y_half[m]

    def put(m, tile):
        y_ref[:, place(m, 1 - core)] = tile

    tiles = [other[:, COL_ORDER.index(q)].astype(jnp.float32).reshape(64, 128) for q in range(16)]
    outgoing_half(left, tiles, right, put)


def incoming_half(core, ref, left, right):
    for b in range(4):
        lanes = slice(128 * b, 128 * b + 128)
        for a, tile in enumerate(swap_groups([both_of(ref, COL_ORDER.index(q))[1] for q in range(4 * b, 4 * b + 4)])):
            right[64 * a : 64 * a + 64, lanes] = tile.astype(jnp.bfloat16)
    for b in range(2):
        lanes = slice(128 * b, 128 * b + 128)
        picks = [both_of(ref, place(m, core))[0] for m in range(4 * b, 4 * b + 4)]
        for a, tile in enumerate(swap_groups(picks)):
            left[64 * a : 64 * a + 64, lanes] = tile.astype(jnp.bfloat16)
    return dot(left[...], right[...], ((0,), (0,)))


def incoming_own(core_ref, own, normed, gate_w, partial, gate, left, right):
    write_gate(normed, gate_w[1], gate)
    partial[...] = incoming_half(core_ref[0], own, left, right)


def incoming_other(core_ref, other, partial, y_ref, left, right):
    product = partial[...] + incoming_half(core_ref[0], other, left, right)
    product = product.reshape(8, 4, 8, 512)
    for b in range(4):
        parts = [product[:, a, :, 128 * b : 128 * b + 128].reshape(64, 128) for a in range(4)]
        write_back(parts, b, y_ref)


def call(kernel, inputs, outputs, scratch, flops):
    smem = [full(pltpu.SMEM) if v.shape == (1,) else full() for v in inputs]
    return pl.pallas_call(
        kernel,
        out_shape=outputs,
        in_specs=smem,
        out_specs=jax.tree.map(lambda _: full(), outputs),
        scratch_shapes=scratch,
        compiler_params=params(),
        cost_estimate=pl.CostEstimate(flops=flops, bytes_accessed=2 << 20, transcendentals=0),
    )(*inputs)


def local(z, gain_in, bias_in, proj, gate_w, gain_out, bias_out, out_w):
    core = lax.axis_index("core").astype(jnp.int32).reshape(1)
    swap = ((0, 1), (1, 0))
    exchange = functools.partial(
        lax.all_to_all,
        axis_name=("yh", "z", "yl", "x"),
        split_axis=0,
        concat_axis=0,
        axis_index_groups=[RANKS],
        tiled=True,
    )
    z4 = z.reshape(4, 8, 32, C)
    shape = jax.ShapeDtypeStruct
    ops_shape = jax.ShapeDtypeStruct((C, 16, 128), jnp.bfloat16)
    normed_shape = shape((8, 128, C), jnp.bfloat16)
    gate_shape = jax.ShapeDtypeStruct((8, 128, C), jnp.float32)
    z_shape = jax.ShapeDtypeStruct((4, 8, 32, C), jnp.float32)
    wide = pltpu.VMEM((16, C, 128), jnp.bfloat16)
    y32 = pltpu.VMEM((8, C, 128), jnp.float32)

    operands = [pltpu.with_memory_space_constraint(v, pltpu.HBM) for v in (z4, gain_in, bias_in, proj, gate_w, gain_out, bias_out)]
    ops, normed, vec, gate_w = pl.pallas_call(
        first_kernel,
        out_shape=(ops_shape, normed_shape, shape((8, C), jnp.float32), shape((2, C, C), jnp.bfloat16)),
        in_specs=[full(pltpu.HBM)] * 7,
        out_specs=(full(), full(), full(), full()),
        scratch_shapes=[
            pltpu.VMEM((4, 8, 32, C), jnp.float32),
            pltpu.VMEM((C, 4 * C), jnp.bfloat16),
            wide,
            pltpu.SemaphoreType.DMA((7,)),
        ],
        compiler_params=params(),
    )(*operands)

    own = exchange(ops).reshape(8, 16, 16, 128)
    other = lax.ppermute(own[:, :, 8:], "core", swap)
    half = 2 * 256 * 256 * 512
    rows = [pltpu.VMEM((8, 32, 512), jnp.float32)]
    outputs = (shape((256, 512), jnp.bfloat16), shape((8, 8, 8, 128), jnp.bfloat16), gate_shape)
    left, y_half, gate = call(outgoing_own, (own, normed, gate_w), outputs, rows, half)
    outputs = shape((8, 16, 8, 128), jnp.bfloat16)
    y = call(outgoing_other, (core, other, left, y_half), outputs, rows, half)
    y = exchange(y.reshape(C, 8, 128))

    z4, ops, normed = pl.pallas_call(
        functools.partial(finish_kernel, 0),
        out_shape=(z_shape, ops_shape, normed_shape),
        in_specs=[full()] * 6,
        out_specs=(full(), full(), full()),
        scratch_shapes=[y32, wide],
        compiler_params=params(),
    )(y, z4, gate, vec, out_w, proj)

    own = exchange(ops).reshape(8, 16, 16, 128)
    other = lax.ppermute(own, "core", swap)
    sides = [pltpu.VMEM((256, 256), jnp.bfloat16), pltpu.VMEM((256, 512), jnp.bfloat16)]
    outputs = (shape((256, 512), jnp.float32), gate_shape)
    partial, gate = call(incoming_own, (core, own, normed, gate_w), outputs, sides, half)
    y = call(incoming_other, (core, other, partial), shape((8, 16, 8, 128), jnp.bfloat16), sides, half)
    y = exchange(y.reshape(C, 8, 128))

    out = pl.pallas_call(
        functools.partial(finish_kernel, 1),
        out_shape=z_shape,
        in_specs=[full()] * 5,
        out_specs=full(pltpu.HBM),
        scratch_shapes=[y32, pltpu.VMEM((4, 8, 32, C), jnp.float32), pltpu.SemaphoreType.DMA((2,))],
        compiler_params=params(),
    )(y, z4, gate, vec, out_w)
    return out.reshape(32, 32, C)


def solution(mesh):
    fine = Mesh(mesh.devices.reshape(2, 4, 2, 2, 8), ("yl", "x", "core", "yh", "z"))
    block = P(("yl", "x", "core"), ("yh", "z"), None)
    return jax.shard_map(
        local,
        mesh=fine,
        in_specs=(block, P(), P(), P(), P(), P(), P(), P()),
        out_specs=block,
        check_vma=False,
    )
```

```python
import functools

import jax
import jax.numpy as jnp
from jax import lax
from jax.experimental import pallas as pl
from jax.experimental.pallas import tpu as pltpu
from jax.sharding import Mesh, PartitionSpec as P

RH_ORDER = (1, 3, 2, 7, 0, 6, 4, 5)
COL_ORDER = (13, 14, 5, 11, 3, 7, 4, 15, 0, 6, 9, 8, 10, 1, 2, 12)
RANKS = [8 * col + rh for rh in RH_ORDER for col in COL_ORDER]
C = 128
EPS = 1e-05
VMEM_LIMIT = 48 * 1024 * 1024


def full(memory_space=pltpu.VMEM):
    return pl.BlockSpec(memory_space=memory_space)


def params():
    return pltpu.CompilerParams(vmem_limit_bytes=VMEM_LIMIT)


def norm_rows(x, gain_row, bias_row):
    centered = x - jnp.mean(x, axis=-1, keepdims=True)
    variance = jnp.mean(centered * centered, axis=-1, keepdims=True)
    return centered * lax.rsqrt(variance + EPS) * gain_row + bias_row


def dot(a, b, contract):
    return lax.dot_general(a, b, (contract, ((), ())), preferred_element_type=jnp.float32)


def emit_operands(z, s, gain_row, bias_row, proj, wide, normed_out):
    rows = z.reshape(256, C)
    normed = norm_rows(rows, gain_row, bias_row).astype(jnp.bfloat16)
    normed_out[s : s + 2] = normed.reshape(2, 128, C)
    projected = dot(proj, normed, ((0,), (1,)))
    left = jax.nn.sigmoid(projected[0:C]) * projected[C : 2 * C]
    right = jax.nn.sigmoid(projected[2 * C : 3 * C]) * projected[3 * C : 4 * C]
    for t in range(2):
        wide[s + t] = left[:, 128 * t : 128 * t + 128].astype(jnp.bfloat16)
        wide[8 + s + t] = right[:, 128 * t : 128 * t + 128].astype(jnp.bfloat16)


def write_gate(normed, gate_w, gate):
    values = dot(normed[...].reshape(1024, C), gate_w, ((1,), (0,)))
    gate[...] = jax.nn.sigmoid(values).reshape(8, 128, C)


def first_kernel(
    z_hbm, gain_in, bias_in, proj_hbm, gate_hbm, gain_out, bias_out,
    ops_ref, normed_ref, vec_ref, gate_w, z, proj, wide, sems,
):
    vectors = (gain_in, bias_in, gain_out, bias_out)
    pairs = [(z_hbm, z), (proj_hbm.at[0], proj)]
    pairs += [(ref, vec_ref.at[2 * i : 2 * i + 2]) for i, ref in enumerate(vectors)]
    pairs += [(gate_hbm, gate_w)]
    copies = [pltpu.make_async_copy(src, dst, sems.at[i]) for i, (src, dst) in enumerate(pairs)]
    for copy in copies:
        copy.start()
    for copy in copies:
        copy.wait()
    for s in range(0, 8, 2):
        rows = jnp.stack([z[:, s], z[:, s + 1]])
        emit_operands(rows, s, vec_ref[0:1], vec_ref[2:3], proj[...], wide, normed_ref)
    ops_ref[...] = jnp.swapaxes(wide[...], 0, 1)


def finish_kernel(layer, y_ref, z_ref, gate_ref, vec, out_w, *rest):
    if layer == 0:
        proj, z_out, ops_ref, normed_out, y32, wide = rest
    else:
        z_hbm, y32, z_out, sems = rest
    y32[...] = jnp.swapaxes(y_ref[...].astype(jnp.float32), 0, 1)
    gain = jnp.transpose(jnp.broadcast_to(vec[4 + layer : 5 + layer, :], (C, C)))
    bias = jnp.transpose(jnp.broadcast_to(vec[6 + layer : 7 + layer, :], (C, C)))
    weight = jnp.concatenate([out_w[layer], out_w[layer]])
    copies = []
    for s in range(0, 8, 2):
        new = []
        for t in (s, s + 1):
            tile = y32[t]
            centered = tile - jnp.mean(tile, axis=0, keepdims=True)
            scale = lax.rsqrt(jnp.mean(centered * centered, axis=0, keepdims=True) + EPS)
            normed = centered * scale * gain + bias
            high = normed.astype(jnp.bfloat16)
            low = (normed - high.astype(jnp.float32)).astype(jnp.bfloat16)
            both = jnp.concatenate([high, low])
            update = gate_ref[t] * dot(both, weight, ((0,), (0,)))
            value = z_ref[:, t] + update.reshape(4, 32, C)
            z_out[:, t] = value
            new.append(value)
        if layer == 0:
            emit_operands(jnp.stack(new), s, vec[1:2], vec[3:4], proj[1], wide, normed_out)
        elif s % 4 == 2:
            part = slice(s - 2, s + 2)
            copies.append(pltpu.make_async_copy(z_out.at[:, part], z_hbm.at[:, part], sems.at[s // 4]))
            copies[-1].start()
    if layer == 0:
        ops_ref[...] = jnp.swapaxes(wide[...], 0, 1)
    for copy in copies:
        copy.wait()


def swap_groups(tiles):
    lane = lax.broadcasted_iota(jnp.int32, tiles[0].shape, 1)
    low = lane < 64
    even = (lane // 32) % 2 == 0
    t0, t1, t2, t3 = tiles
    u0 = jnp.where(low, t0, pltpu.roll(t2, 64, 1))
    u2 = jnp.where(low, pltpu.roll(t0, 64, 1), t2)
    u1 = jnp.where(low, t1, pltpu.roll(t3, 64, 1))
    u3 = jnp.where(low, pltpu.roll(t1, 64, 1), t3)
    v0 = jnp.where(even, u0, pltpu.roll(u1, 32, 1))
    v1 = jnp.where(even, pltpu.roll(u0, 96, 1), u1)
    v2 = jnp.where(even, u2, pltpu.roll(u3, 32, 1))
    v3 = jnp.where(even, pltpu.roll(u2, 96, 1), u3)
    return v0, v1, v2, v3


def write_back(product, b, y_ref):
    for d, tile in enumerate(swap_groups([p.astype(jnp.bfloat16) for p in product])):
        y_ref[:, COL_ORDER.index(4 * b + d)] = tile.reshape(8, 8, 128)


def place(m, parity):
    even, odd = (COL_ORDER.index(2 * RH_ORDER[m] + i) for i in range(2))
    return even + parity * (odd - even)


def both_of(ref, n):
    both = ref[:, n].astype(jnp.float32)
    return both[:, 0:8].reshape(64, 128), both[:, 8:16].reshape(64, 128)


def outgoing_half(left, tiles, right, put):
    for b in range(4):
        for a, tile in enumerate(swap_groups(tiles[4 * b : 4 * b + 4])):
            right[:, 8 * a : 8 * a + 8, 128 * b : 128 * b + 128] = tile.reshape(8, 8, 128)
    rows = right[...].reshape(256, 512).astype(jnp.bfloat16)
    product = dot(left[...], rows, ((1,), (1,)))
    for b in range(2):
        parts = [product[64 * a : 64 * a + 64, 128 * b : 128 * b + 128] for a in range(4)]
        for d, tile in enumerate(swap_groups([p.astype(jnp.bfloat16) for p in parts])):
            put(4 * b + d, tile.reshape(8, 8, 128))


def outgoing_own(own, normed, gate_w, left, y_half, gate, right):
    write_gate(normed, gate_w[0], gate)
    tiles = [both_of(own, COL_ORDER.index(q)) for q in range(16)]
    for b in range(4):
        for a, tile in enumerate(swap_groups([t[0] for t in tiles[4 * b : 4 * b + 4]])):
            left[64 * a : 64 * a + 64, 128 * b : 128 * b + 128] = tile.astype(jnp.bfloat16)

    def put(m, tile):
        y_half[m] = tile

    outgoing_half(left, [t[1] for t in tiles], right, put)


def outgoing_other(core_ref, other, left, y_half, y_ref, right):
    core = core_ref[0]
    for m in range(8):
        y_ref[:, place(m, core)] = y_half[m]

    def put(m, tile):
        y_ref[:, place(m, 1 - core)] = tile

    tiles = [other[:, COL_ORDER.index(q)].astype(jnp.float32).reshape(64, 128) for q in range(16)]
    outgoing_half(left, tiles, right, put)


def incoming_half(core, ref, left, right):
    for b in range(4):
        lanes = slice(128 * b, 128 * b + 128)
        for a, tile in enumerate(swap_groups([both_of(ref, COL_ORDER.index(q))[1] for q in range(4 * b, 4 * b + 4)])):
            right[64 * a : 64 * a + 64, lanes] = tile.astype(jnp.bfloat16)
    for b in range(2):
        lanes = slice(128 * b, 128 * b + 128)
        picks = [both_of(ref, place(m, core))[0] for m in range(4 * b, 4 * b + 4)]
        for a, tile in enumerate(swap_groups(picks)):
            left[64 * a : 64 * a + 64, lanes] = tile.astype(jnp.bfloat16)
    return dot(left[...], right[...], ((0,), (0,)))


def incoming_own(core_ref, own, normed, gate_w, partial, gate, left, right):
    write_gate(normed, gate_w[1], gate)
    partial[...] = incoming_half(core_ref[0], own, left, right)


def incoming_other(core_ref, other, partial, y_ref, left, right):
    product = partial[...] + incoming_half(core_ref[0], other, left, right)
    product = product.reshape(8, 4, 8, 512)
    for b in range(4):
        parts = [product[:, a, :, 128 * b : 128 * b + 128].reshape(64, 128) for a in range(4)]
        write_back(parts, b, y_ref)


def call(kernel, inputs, outputs, scratch, flops):
    smem = [full(pltpu.SMEM) if v.shape == (1,) else full() for v in inputs]
    return pl.pallas_call(
        kernel,
        out_shape=outputs,
        in_specs=smem,
        out_specs=jax.tree.map(lambda _: full(), outputs),
        scratch_shapes=scratch,
        compiler_params=params(),
        cost_estimate=pl.CostEstimate(flops=flops, bytes_accessed=2 << 20, transcendentals=0),
    )(*inputs)


def local(z, gain_in, bias_in, proj, gate_w, gain_out, bias_out, out_w):
    core = lax.axis_index("core").astype(jnp.int32).reshape(1)
    swap = ((0, 1), (1, 0))
    exchange = functools.partial(
        lax.all_to_all,
        axis_name=("yh", "z", "yl", "x"),
        split_axis=0,
        concat_axis=0,
        axis_index_groups=[RANKS],
        tiled=True,
    )
    z4 = z.reshape(4, 8, 32, C)
    shape = jax.ShapeDtypeStruct
    ops_shape = jax.ShapeDtypeStruct((C, 16, 128), jnp.bfloat16)
    normed_shape = shape((8, 128, C), jnp.bfloat16)
    gate_shape = jax.ShapeDtypeStruct((8, 128, C), jnp.float32)
    z_shape = jax.ShapeDtypeStruct((4, 8, 32, C), jnp.float32)
    wide = pltpu.VMEM((16, C, 128), jnp.bfloat16)
    y32 = pltpu.VMEM((8, C, 128), jnp.float32)

    operands = [pltpu.with_memory_space_constraint(v, pltpu.HBM) for v in (z4, gain_in, bias_in, proj, gate_w, gain_out, bias_out)]
    ops, normed, vec, gate_w = pl.pallas_call(
        first_kernel,
        out_shape=(ops_shape, normed_shape, shape((8, C), jnp.float32), shape((2, C, C), jnp.bfloat16)),
        in_specs=[full(pltpu.HBM)] * 7,
        out_specs=(full(), full(), full(), full()),
        scratch_shapes=[
            pltpu.VMEM((4, 8, 32, C), jnp.float32),
            pltpu.VMEM((C, 4 * C), jnp.bfloat16),
            wide,
            pltpu.SemaphoreType.DMA((7,)),
        ],
        compiler_params=params(),
    )(*operands)

    own = exchange(ops).reshape(8, 16, 16, 128)
    other = lax.ppermute(own[:, :, 8:], "core", swap)
    half = 2 * 256 * 256 * 512
    rows = [pltpu.VMEM((8, 32, 512), jnp.float32)]
    outputs = (shape((256, 512), jnp.bfloat16), shape((8, 8, 8, 128), jnp.bfloat16), gate_shape)
    left, y_half, gate = call(outgoing_own, (own, normed, gate_w), outputs, rows, half)
    outputs = shape((8, 16, 8, 128), jnp.bfloat16)
    y = call(outgoing_other, (core, other, left, y_half), outputs, rows, half)
    y = exchange(y.reshape(C, 8, 128))

    z4, ops, normed = pl.pallas_call(
        functools.partial(finish_kernel, 0),
        out_shape=(z_shape, ops_shape, normed_shape),
        in_specs=[full()] * 6,
        out_specs=(full(), full(), full()),
        scratch_shapes=[y32, wide],
        compiler_params=params(),
    )(y, z4, gate, vec, out_w, proj)

    own = exchange(ops).reshape(8, 16, 16, 128)
    other = lax.ppermute(own, "core", swap)
    sides = [pltpu.VMEM((256, 256), jnp.bfloat16), pltpu.VMEM((256, 512), jnp.bfloat16)]
    outputs = (shape((256, 512), jnp.float32), gate_shape)
    partial, gate = call(incoming_own, (core, own, normed, gate_w), outputs, sides, half)
    y = call(incoming_other, (core, other, partial), shape((8, 16, 8, 128), jnp.bfloat16), sides, half)
    y = exchange(y.reshape(C, 8, 128))

    out = pl.pallas_call(
        functools.partial(finish_kernel, 1),
        out_shape=z_shape,
        in_specs=[full()] * 5,
        out_specs=full(pltpu.HBM),
        scratch_shapes=[y32, pltpu.VMEM((4, 8, 32, C), jnp.float32), pltpu.SemaphoreType.DMA((2,))],
        compiler_params=params(),
    )(y, z4, gate, vec, out_w)
    return out.reshape(32, 32, C)


def solution(mesh):
    fine = Mesh(mesh.devices.reshape(2, 4, 2, 2, 8), ("yl", "x", "core", "yh", "z"))
    block = P(("yl", "x", "core"), ("yh", "z"), None)
    return jax.shard_map(
        local,
        mesh=fine,
        in_specs=(block, P(), P(), P(), P(), P(), P(), P()),
        out_specs=block,
        check_vma=False,
    )
```

```python
import functools

import jax
import jax.numpy as jnp
from jax import lax
from jax.experimental import pallas as pl
from jax.experimental.pallas import tpu as pltpu
from jax.sharding import Mesh, PartitionSpec as P

RH_ORDER = (1, 3, 2, 7, 0, 6, 4, 5)
COL_ORDER = (13, 14, 5, 11, 3, 7, 4, 15, 0, 6, 9, 8, 10, 1, 2, 12)
RANKS = [8 * col + rh for rh in RH_ORDER for col in COL_ORDER]
SENT = (jnp.float32, jnp.bfloat16)
C = 128
EPS = 1e-05
VMEM_LIMIT = 48 * 1024 * 1024


def full(memory_space=pltpu.VMEM):
    return pl.BlockSpec(memory_space=memory_space)


def params():
    return pltpu.CompilerParams(vmem_limit_bytes=VMEM_LIMIT)


def norm_rows(x, gain_row, bias_row):
    centered = x - jnp.mean(x, axis=-1, keepdims=True)
    variance = jnp.mean(centered * centered, axis=-1, keepdims=True)
    return centered * lax.rsqrt(variance + EPS) * gain_row + bias_row


def dot(a, b, contract):
    return lax.dot_general(a, b, (contract, ((), ())), preferred_element_type=jnp.float32)


def emit_operands(z, s, gain_row, bias_row, proj, wide, normed_out):
    rows = z.reshape(256, C)
    normed = norm_rows(rows, gain_row, bias_row).astype(jnp.bfloat16)
    normed_out[s : s + 2] = normed.reshape(2, 128, C)
    projected = dot(proj, normed, ((0,), (1,)))
    left = jax.nn.sigmoid(projected[0:C]) * projected[C : 2 * C]
    right = jax.nn.sigmoid(projected[2 * C : 3 * C]) * projected[3 * C : 4 * C]
    for t in range(2):
        wide[s + t] = left[:, 128 * t : 128 * t + 128].astype(jnp.bfloat16)
        wide[8 + s + t] = right[:, 128 * t : 128 * t + 128].astype(jnp.bfloat16)


def write_gate(normed, gate_w, gate):
    values = dot(normed[...].reshape(1024, C), gate_w, ((1,), (0,)))
    gate[...] = jax.nn.sigmoid(values).reshape(8, 128, C)


def first_kernel(
    z_hbm, gain_in, bias_in, proj_hbm, gate_hbm, gain_out, bias_out,
    ops_ref, normed_ref, vec_ref, gate_w, z, proj, wide, sems,
):
    vectors = (gain_in, bias_in, gain_out, bias_out)
    pairs = [(z_hbm, z), (proj_hbm.at[0], proj)]
    pairs += [(ref, vec_ref.at[2 * i : 2 * i + 2]) for i, ref in enumerate(vectors)]
    pairs += [(gate_hbm, gate_w)]
    copies = [pltpu.make_async_copy(src, dst, sems.at[i]) for i, (src, dst) in enumerate(pairs)]
    for copy in copies:
        copy.start()
    for copy in copies:
        copy.wait()
    for s in range(0, 8, 2):
        rows = jnp.stack([z[:, s], z[:, s + 1]])
        emit_operands(rows, s, vec_ref[0:1], vec_ref[2:3], proj[...], wide, normed_ref)
    ops_ref[...] = jnp.swapaxes(wide[...], 0, 1)


def finish_kernel(layer, y_ref, z_ref, gate_ref, vec, out_w, *rest):
    if layer == 0:
        proj, z_out, ops_ref, normed_out, y32, wide = rest
    else:
        z_hbm, y32, z_out, sems = rest
    y32[...] = jnp.swapaxes(y_ref[...].astype(jnp.float32), 0, 1)
    gain = jnp.transpose(jnp.broadcast_to(vec[4 + layer : 5 + layer, :], (C, C)))
    bias = jnp.transpose(jnp.broadcast_to(vec[6 + layer : 7 + layer, :], (C, C)))
    weight = out_w[layer]
    if SENT[layer] == jnp.bfloat16:
        weight = jnp.concatenate([weight, weight])
    copies = []
    for s in range(0, 8, 2):
        new = []
        for t in (s, s + 1):
            tile = y32[t]
            centered = tile - jnp.mean(tile, axis=0, keepdims=True)
            scale = lax.rsqrt(jnp.mean(centered * centered, axis=0, keepdims=True) + EPS)
            normed = centered * scale * gain + bias
            parts = [normed.astype(jnp.bfloat16)]
            if SENT[layer] == jnp.bfloat16:
                parts.append((normed - parts[0].astype(jnp.float32)).astype(jnp.bfloat16))
            update = gate_ref[t] * dot(jnp.concatenate(parts), weight, ((0,), (0,)))
            value = z_ref[:, t] + update.reshape(4, 32, C)
            z_out[:, t] = value
            new.append(value)
        if layer == 0:
            emit_operands(jnp.stack(new), s, vec[1:2], vec[3:4], proj[1], wide, normed_out)
        elif s % 4 == 2:
            part = slice(s - 2, s + 2)
            copies.append(pltpu.make_async_copy(z_out.at[:, part], z_hbm.at[:, part], sems.at[s // 4]))
            copies[-1].start()
    if layer == 0:
        ops_ref[...] = jnp.swapaxes(wide[...], 0, 1)
    for copy in copies:
        copy.wait()


def swap_groups(tiles):
    lane = lax.broadcasted_iota(jnp.int32, tiles[0].shape, 1)
    low = lane < 64
    even = (lane // 32) % 2 == 0
    t0, t1, t2, t3 = tiles
    u0 = jnp.where(low, t0, pltpu.roll(t2, 64, 1))
    u2 = jnp.where(low, pltpu.roll(t0, 64, 1), t2)
    u1 = jnp.where(low, t1, pltpu.roll(t3, 64, 1))
    u3 = jnp.where(low, pltpu.roll(t1, 64, 1), t3)
    v0 = jnp.where(even, u0, pltpu.roll(u1, 32, 1))
    v1 = jnp.where(even, pltpu.roll(u0, 96, 1), u1)
    v2 = jnp.where(even, u2, pltpu.roll(u3, 32, 1))
    v3 = jnp.where(even, pltpu.roll(u2, 96, 1), u3)
    return v0, v1, v2, v3


def write_back(product, b, y_ref):
    for d, tile in enumerate(swap_groups([p.astype(y_ref.dtype) for p in product])):
        y_ref[:, COL_ORDER.index(4 * b + d)] = tile.reshape(8, 8, 128)


def place(m, parity):
    even, odd = (COL_ORDER.index(2 * RH_ORDER[m] + i) for i in range(2))
    return even + parity * (odd - even)


def both_of(ref, n):
    both = ref[:, n].astype(jnp.float32)
    return both[:, 0:8].reshape(64, 128), both[:, 8:16].reshape(64, 128)


def outgoing_half(left, tiles, right, put):
    for b in range(4):
        for a, tile in enumerate(swap_groups(tiles[4 * b : 4 * b + 4])):
            right[:, 8 * a : 8 * a + 8, 128 * b : 128 * b + 128] = tile.reshape(8, 8, 128)
    rows = right[...].reshape(256, 512).astype(jnp.bfloat16)
    product = dot(left[...], rows, ((1,), (1,)))
    for b in range(2):
        parts = [product[64 * a : 64 * a + 64, 128 * b : 128 * b + 128] for a in range(4)]
        for d, tile in enumerate(swap_groups([p.astype(SENT[0]) for p in parts])):
            put(4 * b + d, tile.reshape(8, 8, 128))


def outgoing_own(own, normed, gate_w, left, y_half, gate, right):
    write_gate(normed, gate_w[0], gate)
    tiles = [both_of(own, COL_ORDER.index(q)) for q in range(16)]
    for b in range(4):
        for a, tile in enumerate(swap_groups([t[0] for t in tiles[4 * b : 4 * b + 4]])):
            left[64 * a : 64 * a + 64, 128 * b : 128 * b + 128] = tile.astype(jnp.bfloat16)

    def put(m, tile):
        y_half[m] = tile

    outgoing_half(left, [t[1] for t in tiles], right, put)


def outgoing_other(core_ref, other, left, y_half, y_ref, right):
    core = core_ref[0]
    for m in range(8):
        y_ref[:, place(m, core)] = y_half[m]

    def put(m, tile):
        y_ref[:, place(m, 1 - core)] = tile

    tiles = [other[:, COL_ORDER.index(q)].astype(jnp.float32).reshape(64, 128) for q in range(16)]
    outgoing_half(left, tiles, right, put)


def incoming_half(core, ref, left, right):
    for b in range(4):
        lanes = slice(128 * b, 128 * b + 128)
        for a, tile in enumerate(swap_groups([both_of(ref, COL_ORDER.index(q))[1] for q in range(4 * b, 4 * b + 4)])):
            right[64 * a : 64 * a + 64, lanes] = tile.astype(jnp.bfloat16)
    for b in range(2):
        lanes = slice(128 * b, 128 * b + 128)
        picks = [both_of(ref, place(m, core))[0] for m in range(4 * b, 4 * b + 4)]
        for a, tile in enumerate(swap_groups(picks)):
            left[64 * a : 64 * a + 64, lanes] = tile.astype(jnp.bfloat16)
    return dot(left[...], right[...], ((0,), (0,)))


def incoming_own(core_ref, own, normed, gate_w, partial, gate, left, right):
    write_gate(normed, gate_w[1], gate)
    partial[...] = incoming_half(core_ref[0], own, left, right)


def incoming_other(core_ref, other, partial, y_ref, left, right):
    product = partial[...] + incoming_half(core_ref[0], other, left, right)
    product = product.reshape(8, 4, 8, 512)
    for b in range(4):
        parts = [product[:, a, :, 128 * b : 128 * b + 128].reshape(64, 128) for a in range(4)]
        write_back(parts, b, y_ref)


def call(kernel, inputs, outputs, scratch, flops):
    smem = [full(pltpu.SMEM) if v.shape == (1,) else full() for v in inputs]
    return pl.pallas_call(
        kernel,
        out_shape=outputs,
        in_specs=smem,
        out_specs=jax.tree.map(lambda _: full(), outputs),
        scratch_shapes=scratch,
        compiler_params=params(),
        cost_estimate=pl.CostEstimate(flops=flops, bytes_accessed=2 << 20, transcendentals=0),
    )(*inputs)


def local(z, gain_in, bias_in, proj, gate_w, gain_out, bias_out, out_w):
    core = lax.axis_index("core").astype(jnp.int32).reshape(1)
    swap = ((0, 1), (1, 0))
    exchange = functools.partial(
        lax.all_to_all,
        axis_name=("yh", "z", "yl", "x"),
        split_axis=0,
        concat_axis=0,
        axis_index_groups=[RANKS],
        tiled=True,
    )
    z4 = z.reshape(4, 8, 32, C)
    shape = jax.ShapeDtypeStruct
    ops_shape = jax.ShapeDtypeStruct((C, 16, 128), jnp.bfloat16)
    normed_shape = shape((8, 128, C), jnp.bfloat16)
    gate_shape = jax.ShapeDtypeStruct((8, 128, C), jnp.float32)
    z_shape = jax.ShapeDtypeStruct((4, 8, 32, C), jnp.float32)
    wide = pltpu.VMEM((16, C, 128), jnp.bfloat16)
    y32 = pltpu.VMEM((8, C, 128), jnp.float32)

    operands = [pltpu.with_memory_space_constraint(v, pltpu.HBM) for v in (z4, gain_in, bias_in, proj, gate_w, gain_out, bias_out)]
    ops, normed, vec, gate_w = pl.pallas_call(
        first_kernel,
        out_shape=(ops_shape, normed_shape, shape((8, C), jnp.float32), shape((2, C, C), jnp.bfloat16)),
        in_specs=[full(pltpu.HBM)] * 7,
        out_specs=(full(), full(), full(), full()),
        scratch_shapes=[
            pltpu.VMEM((4, 8, 32, C), jnp.float32),
            pltpu.VMEM((C, 4 * C), jnp.bfloat16),
            wide,
            pltpu.SemaphoreType.DMA((7,)),
        ],
        compiler_params=params(),
    )(*operands)

    own = exchange(ops).reshape(8, 16, 16, 128)
    other = lax.ppermute(own[:, :, 8:], "core", swap)
    half = 2 * 256 * 256 * 512
    rows = [pltpu.VMEM((8, 32, 512), jnp.float32)]
    outputs = (shape((256, 512), jnp.bfloat16), shape((8, 8, 8, 128), SENT[0]), gate_shape)
    left, y_half, gate = call(outgoing_own, (own, normed, gate_w), outputs, rows, half)
    outputs = shape((8, 16, 8, 128), SENT[0])
    y = call(outgoing_other, (core, other, left, y_half), outputs, rows, half)
    y = exchange(y.reshape(C, 8, 128))

    z4, ops, normed = pl.pallas_call(
        functools.partial(finish_kernel, 0),
        out_shape=(z_shape, ops_shape, normed_shape),
        in_specs=[full()] * 6,
        out_specs=(full(), full(), full()),
        scratch_shapes=[y32, wide],
        compiler_params=params(),
    )(y, z4, gate, vec, out_w, proj)

    own = exchange(ops).reshape(8, 16, 16, 128)
    other = lax.ppermute(own, "core", swap)
    sides = [pltpu.VMEM((256, 256), jnp.bfloat16), pltpu.VMEM((256, 512), jnp.bfloat16)]
    outputs = (shape((256, 512), jnp.float32), gate_shape)
    partial, gate = call(incoming_own, (core, own, normed, gate_w), outputs, sides, half)
    y = call(incoming_other, (core, other, partial), shape((8, 16, 8, 128), SENT[1]), sides, half)
    y = exchange(y.reshape(C, 8, 128))

    out = pl.pallas_call(
        functools.partial(finish_kernel, 1),
        out_shape=z_shape,
        in_specs=[full()] * 5,
        out_specs=full(pltpu.HBM),
        scratch_shapes=[y32, pltpu.VMEM((4, 8, 32, C), jnp.float32), pltpu.SemaphoreType.DMA((2,))],
        compiler_params=params(),
    )(y, z4, gate, vec, out_w)
    return out.reshape(32, 32, C)


def solution(mesh):
    fine = Mesh(mesh.devices.reshape(2, 4, 2, 2, 8), ("yl", "x", "core", "yh", "z"))
    block = P(("yl", "x", "core"), ("yh", "z"), None)
    return jax.shard_map(
        local,
        mesh=fine,
        in_specs=(block, P(), P(), P(), P(), P(), P(), P()),
        out_specs=block,
        check_vma=False,
    )
```

```python
import functools

import jax
import jax.numpy as jnp
from jax import lax
from jax.experimental import pallas as pl
from jax.experimental.pallas import tpu as pltpu
from jax.sharding import Mesh, PartitionSpec as P

RH_ORDER = (1, 3, 7, 2, 6, 0, 4, 5)
COL_ORDER = (13, 14, 5, 11, 3, 7, 4, 15, 0, 6, 9, 8, 10, 1, 2, 12)
RANKS = [8 * col + rh for rh in RH_ORDER for col in COL_ORDER]
SENT = (jnp.float32, jnp.bfloat16)
C = 128
EPS = 1e-05
VMEM_LIMIT = 48 * 1024 * 1024


def full(memory_space=pltpu.VMEM):
    return pl.BlockSpec(memory_space=memory_space)


def params():
    return pltpu.CompilerParams(vmem_limit_bytes=VMEM_LIMIT)


def norm_rows(x, gain_row, bias_row):
    centered = x - jnp.mean(x, axis=-1, keepdims=True)
    variance = jnp.mean(centered * centered, axis=-1, keepdims=True)
    return centered * lax.rsqrt(variance + EPS) * gain_row + bias_row


def dot(a, b, contract):
    return lax.dot_general(a, b, (contract, ((), ())), preferred_element_type=jnp.float32)


def emit_operands(z, s, gain_row, bias_row, proj, wide, normed_out):
    rows = z.reshape(256, C)
    normed = norm_rows(rows, gain_row, bias_row).astype(jnp.bfloat16)
    normed_out[s : s + 2] = normed.reshape(2, 128, C)
    projected = dot(proj, normed, ((0,), (1,)))
    left = jax.nn.sigmoid(projected[0:C]) * projected[C : 2 * C]
    right = jax.nn.sigmoid(projected[2 * C : 3 * C]) * projected[3 * C : 4 * C]
    for t in range(2):
        wide[s + t] = left[:, 128 * t : 128 * t + 128].astype(jnp.bfloat16)
        wide[8 + s + t] = right[:, 128 * t : 128 * t + 128].astype(jnp.bfloat16)


def write_gate(normed, gate_w, gate):
    values = dot(normed[...].reshape(1024, C), gate_w, ((1,), (0,)))
    gate[...] = jax.nn.sigmoid(values).reshape(8, 128, C)


def first_kernel(
    z_hbm, gain_in, bias_in, proj_hbm, gate_hbm, gain_out, bias_out,
    ops_ref, normed_ref, vec_ref, gate_w, z, proj, wide, sems,
):
    vectors = (gain_in, bias_in, gain_out, bias_out)
    pairs = [(z_hbm, z), (proj_hbm.at[0], proj)]
    pairs += [(ref, vec_ref.at[2 * i : 2 * i + 2]) for i, ref in enumerate(vectors)]
    pairs += [(gate_hbm, gate_w)]
    copies = [pltpu.make_async_copy(src, dst, sems.at[i]) for i, (src, dst) in enumerate(pairs)]
    for copy in copies:
        copy.start()
    for copy in copies[:4]:
        copy.wait()
    for s in range(0, 8, 2):
        rows = jnp.stack([z[:, s], z[:, s + 1]])
        emit_operands(rows, s, vec_ref[0:1], vec_ref[2:3], proj[...], wide, normed_ref)
    ops_ref[...] = jnp.swapaxes(wide[...], 0, 1)
    for copy in copies[4:]:
        copy.wait()


def finish_kernel(layer, y_ref, z_ref, gate_ref, vec, out_w, *rest):
    if layer == 0:
        proj, z_out, ops_ref, normed_out, y32, wide = rest
    else:
        z_hbm, y32, z_out, sems = rest
    y32[...] = jnp.swapaxes(y_ref[...].astype(jnp.float32), 0, 1)
    gain = jnp.transpose(jnp.broadcast_to(vec[4 + layer : 5 + layer, :], (C, C)))
    bias = jnp.transpose(jnp.broadcast_to(vec[6 + layer : 7 + layer, :], (C, C)))
    weight = out_w[layer]
    if SENT[layer] == jnp.bfloat16:
        weight = jnp.concatenate([weight, weight])
    copies = []
    for s in range(0, 8, 2):
        new = []
        for t in (s, s + 1):
            tile = y32[t]
            centered = tile - jnp.mean(tile, axis=0, keepdims=True)
            scale = lax.rsqrt(jnp.mean(centered * centered, axis=0, keepdims=True) + EPS)
            normed = centered * scale * gain + bias
            parts = [normed.astype(jnp.bfloat16)]
            if SENT[layer] == jnp.bfloat16:
                parts.append((normed - parts[0].astype(jnp.float32)).astype(jnp.bfloat16))
            update = gate_ref[t] * dot(jnp.concatenate(parts), weight, ((0,), (0,)))
            value = z_ref[:, t] + update.reshape(4, 32, C)
            z_out[:, t] = value
            new.append(value)
        if layer == 0:
            emit_operands(jnp.stack(new), s, vec[1:2], vec[3:4], proj[1], wide, normed_out)
        elif s % 4 == 2:
            part = slice(s - 2, s + 2)
            copies.append(pltpu.make_async_copy(z_out.at[:, part], z_hbm.at[:, part], sems.at[s // 4]))
            copies[-1].start()
    if layer == 0:
        ops_ref[...] = jnp.swapaxes(wide[...], 0, 1)
    for copy in copies:
        copy.wait()


def swap_groups(tiles):
    lane = lax.broadcasted_iota(jnp.int32, tiles[0].shape, 1)
    low = lane < 64
    even = (lane // 32) % 2 == 0
    t0, t1, t2, t3 = tiles
    u0 = jnp.where(low, t0, pltpu.roll(t2, 64, 1))
    u2 = jnp.where(low, pltpu.roll(t0, 64, 1), t2)
    u1 = jnp.where(low, t1, pltpu.roll(t3, 64, 1))
    u3 = jnp.where(low, pltpu.roll(t1, 64, 1), t3)
    v0 = jnp.where(even, u0, pltpu.roll(u1, 32, 1))
    v1 = jnp.where(even, pltpu.roll(u0, 96, 1), u1)
    v2 = jnp.where(even, u2, pltpu.roll(u3, 32, 1))
    v3 = jnp.where(even, pltpu.roll(u2, 96, 1), u3)
    return v0, v1, v2, v3


def write_back(product, b, y_ref):
    for d, tile in enumerate(swap_groups([p.astype(y_ref.dtype) for p in product])):
        y_ref[:, COL_ORDER.index(4 * b + d)] = tile.reshape(8, 8, 128)


def place(m, parity):
    even, odd = (COL_ORDER.index(2 * RH_ORDER[m] + i) for i in range(2))
    return even + parity * (odd - even)


def both_of(ref, n):
    both = ref[:, n].astype(jnp.float32)
    return both[:, 0:8].reshape(64, 128), both[:, 8:16].reshape(64, 128)


def outgoing_half(left, tiles, right, put):
    for b in range(4):
        for a, tile in enumerate(swap_groups(tiles[4 * b : 4 * b + 4])):
            right[:, 8 * a : 8 * a + 8, 128 * b : 128 * b + 128] = tile.reshape(8, 8, 128)
    rows = right[...].reshape(256, 512).astype(jnp.bfloat16)
    product = dot(left[...], rows, ((1,), (1,)))
    for b in range(2):
        parts = [product[64 * a : 64 * a + 64, 128 * b : 128 * b + 128] for a in range(4)]
        for d, tile in enumerate(swap_groups([p.astype(SENT[0]) for p in parts])):
            put(4 * b + d, tile.reshape(8, 8, 128))


def outgoing_own(own, normed, gate_w, left, y_half, gate, right):
    write_gate(normed, gate_w[0], gate)
    tiles = [both_of(own, COL_ORDER.index(q)) for q in range(16)]
    for b in range(4):
        for a, tile in enumerate(swap_groups([t[0] for t in tiles[4 * b : 4 * b + 4]])):
            left[64 * a : 64 * a + 64, 128 * b : 128 * b + 128] = tile.astype(jnp.bfloat16)

    def put(m, tile):
        y_half[m] = tile

    outgoing_half(left, [t[1] for t in tiles], right, put)


def outgoing_other(core_ref, other, left, y_half, y_ref, right):
    core = core_ref[0]
    for m in range(8):
        y_ref[:, place(m, core)] = y_half[m]

    def put(m, tile):
        y_ref[:, place(m, 1 - core)] = tile

    tiles = [other[:, COL_ORDER.index(q)].astype(jnp.float32).reshape(64, 128) for q in range(16)]
    outgoing_half(left, tiles, right, put)


def incoming_half(core, ref, left, right):
    for b in range(4):
        lanes = slice(128 * b, 128 * b + 128)
        for a, tile in enumerate(swap_groups([both_of(ref, COL_ORDER.index(q))[1] for q in range(4 * b, 4 * b + 4)])):
            right[64 * a : 64 * a + 64, lanes] = tile.astype(jnp.bfloat16)
    for b in range(2):
        lanes = slice(128 * b, 128 * b + 128)
        picks = [both_of(ref, place(m, core))[0] for m in range(4 * b, 4 * b + 4)]
        for a, tile in enumerate(swap_groups(picks)):
            left[64 * a : 64 * a + 64, lanes] = tile.astype(jnp.bfloat16)
    return dot(left[...], right[...], ((0,), (0,)))


def incoming_own(core_ref, own, normed, gate_w, partial, gate, left, right):
    write_gate(normed, gate_w[1], gate)
    partial[...] = incoming_half(core_ref[0], own, left, right)


def incoming_other(core_ref, other, partial, y_ref, left, right):
    product = partial[...] + incoming_half(core_ref[0], other, left, right)
    product = product.reshape(8, 4, 8, 512)
    for b in range(4):
        parts = [product[:, a, :, 128 * b : 128 * b + 128].reshape(64, 128) for a in range(4)]
        write_back(parts, b, y_ref)


def call(kernel, inputs, outputs, scratch, flops):
    smem = [full(pltpu.SMEM) if v.shape == (1,) else full() for v in inputs]
    return pl.pallas_call(
        kernel,
        out_shape=outputs,
        in_specs=smem,
        out_specs=jax.tree.map(lambda _: full(), outputs),
        scratch_shapes=scratch,
        compiler_params=params(),
        cost_estimate=pl.CostEstimate(flops=flops, bytes_accessed=2 << 20, transcendentals=0),
    )(*inputs)


def local(z, gain_in, bias_in, proj, gate_w, gain_out, bias_out, out_w):
    core = lax.axis_index("core").astype(jnp.int32).reshape(1)
    swap = ((0, 1), (1, 0))
    exchange = functools.partial(
        lax.all_to_all,
        axis_name=("yh", "z", "yl", "x"),
        split_axis=0,
        concat_axis=0,
        axis_index_groups=[RANKS],
        tiled=True,
    )
    z4 = z.reshape(4, 8, 32, C)
    shape = jax.ShapeDtypeStruct
    ops_shape = jax.ShapeDtypeStruct((C, 16, 128), jnp.bfloat16)
    normed_shape = shape((8, 128, C), jnp.bfloat16)
    gate_shape = jax.ShapeDtypeStruct((8, 128, C), jnp.float32)
    z_shape = jax.ShapeDtypeStruct((4, 8, 32, C), jnp.float32)
    wide = pltpu.VMEM((16, C, 128), jnp.bfloat16)
    y32 = pltpu.VMEM((8, C, 128), jnp.float32)

    operands = [pltpu.with_memory_space_constraint(v, pltpu.HBM) for v in (z4, gain_in, bias_in, proj, gate_w, gain_out, bias_out)]
    ops, normed, vec, gate_w = pl.pallas_call(
        first_kernel,
        out_shape=(ops_shape, normed_shape, shape((8, C), jnp.float32), shape((2, C, C), jnp.bfloat16)),
        in_specs=[full(pltpu.HBM)] * 7,
        out_specs=(full(), full(), full(), full()),
        scratch_shapes=[
            pltpu.VMEM((4, 8, 32, C), jnp.float32),
            pltpu.VMEM((C, 4 * C), jnp.bfloat16),
            wide,
            pltpu.SemaphoreType.DMA((7,)),
        ],
        compiler_params=params(),
    )(*operands)

    own = exchange(ops).reshape(8, 16, 16, 128)
    other = lax.ppermute(own[:, :, 8:], "core", swap)
    half = 2 * 256 * 256 * 512
    rows = [pltpu.VMEM((8, 32, 512), jnp.float32)]
    outputs = (shape((256, 512), jnp.bfloat16), shape((8, 8, 8, 128), SENT[0]), gate_shape)
    left, y_half, gate = call(outgoing_own, (own, normed, gate_w), outputs, rows, half)
    outputs = shape((8, 16, 8, 128), SENT[0])
    y = call(outgoing_other, (core, other, left, y_half), outputs, rows, half)
    y = exchange(y.reshape(C, 8, 128))

    z4, ops, normed = pl.pallas_call(
        functools.partial(finish_kernel, 0),
        out_shape=(z_shape, ops_shape, normed_shape),
        in_specs=[full()] * 6,
        out_specs=(full(), full(), full()),
        scratch_shapes=[y32, wide],
        compiler_params=params(),
    )(y, z4, gate, vec, out_w, proj)

    own = exchange(ops).reshape(8, 16, 16, 128)
    other = lax.ppermute(own, "core", swap)
    sides = [pltpu.VMEM((256, 256), jnp.bfloat16), pltpu.VMEM((256, 512), jnp.bfloat16)]
    outputs = (shape((256, 512), jnp.float32), gate_shape)
    partial, gate = call(incoming_own, (core, own, normed, gate_w), outputs, sides, half)
    y = call(incoming_other, (core, other, partial), shape((8, 16, 8, 128), SENT[1]), sides, half)
    y = exchange(y.reshape(C, 8, 128))

    out = pl.pallas_call(
        functools.partial(finish_kernel, 1),
        out_shape=z_shape,
        in_specs=[full()] * 5,
        out_specs=full(pltpu.HBM),
        scratch_shapes=[y32, pltpu.VMEM((4, 8, 32, C), jnp.float32), pltpu.SemaphoreType.DMA((2,))],
        compiler_params=params(),
    )(y, z4, gate, vec, out_w)
    return out.reshape(32, 32, C)


def solution(mesh):
    fine = Mesh(mesh.devices.reshape(2, 4, 2, 2, 8), ("yl", "x", "core", "yh", "z"))
    block = P(("yl", "x", "core"), ("yh", "z"), None)
    return jax.shard_map(
        local,
        mesh=fine,
        in_specs=(block, P(), P(), P(), P(), P(), P(), P()),
        out_specs=block,
        check_vma=False,
    )
```
